256 devices in a mesh: state: 8 (over z_lo, y), slab: 32 (over z_hi, x, core).
Axes of the slice: x: 4, y: 4, z: 8 (z_hi: 4, z_lo: 2; z = z_hi * 2 + z_lo), core: 2. Of those that a mesh axis runs over, the one named last changes fastest.
Arguments:
- state_images: bfloat16 [8, 2, 320, 2, 320, 128], P('state', None, 'slab'), may hold values from -6 to 6
- rot_index: int32 [8], P('state'), may hold values from 0 to 31
- counts: int32 [8], P('state'), may hold values from 16 to 64
Outputs:
- combined: float32 [2, 320, 2, 320, 128], P(None, 'slab', None, None, 'state')
The draws below stay inside these ranges and needn't reach their ends.
All inputs are finite; a program needn't handle non-finite values.
Results may differ from the reference program's by a relative error of at most 0.022.
Values may be sent and summed in bfloat16 or wider, within the bound.
A program may use at most 192 MiB of HBM per device.

```python
import math
import jax
import jax.numpy as jnp
from jax import lax

NX = 320
NZ = 320
NY = 128
COEF = 2
ANGLES = 32
STATES = 8


def touch_ends(drawn, own_key, smallest, high):
    index_at = [jax.random.randint(jax.random.fold_in(own_key, axis), (), 0, length) for axis, length in enumerate(drawn.shape)]
    widest = drawn.shape.index(max(drawn.shape))
    neighbour = index_at[:widest] + [(index_at[widest] + 1) % drawn.shape[widest]] + index_at[widest + 1:]
    return drawn.at[tuple(index_at)].set(smallest).at[tuple(neighbour)].set(high)


def block_levels(key, dims, pieces, least, high):
    level = 1.0
    for dim, shards_of in pieces:
        steps = jax.random.uniform(jax.random.fold_in(jax.random.fold_in(key, 6), dim), (shards_of,), jnp.float32, least / len(pieces), high / len(pieces))
        level = level * jnp.repeat(jnp.exp(steps), dims[dim] // shards_of).reshape((-1,) + (1,) * (len(dims) - 1 - dim))
    return level


def normal_values(rng, shape, deviation, limit, split=(), kind=jnp.bfloat16):
    gain = block_levels(rng, shape, split, -0.22, 0.18) if split else 1.0
    entries = jax.random.normal(rng, shape, jnp.float32) * deviation * gain
    return jnp.minimum(jnp.maximum(entries, -limit), limit).astype(kind)


def setup_inputs(seed: int = 0) -> dict:
    arg_keys = jax.random.split(jax.random.key(seed), 4)
    return {
        "state_images": normal_values(arg_keys[0], (STATES, COEF, NZ, 2, NX, NY), 1.0, 6.0, ((0, 8), (2, 32))),
        "rot_index": touch_ends(jax.random.randint(arg_keys[1], (STATES,), 0, ANGLES), jax.random.fold_in(arg_keys[1], 1), 0, ANGLES - 1).astype(jnp.int32),
        "counts": touch_ends(jax.random.randint(arg_keys[2], (STATES,), 16, 65), jax.random.fold_in(arg_keys[2], 1), 16, 64).astype(jnp.int32),
    }


angle_step = math.pi / 120.0
count_scale = 1.0 / 64.0


def dft_tables(length):
    points = jnp.arange(length, dtype=jnp.int32)
    phases = ((points[:, None] * points[None, :]) % length).astype(jnp.float32) * (2.0 * math.pi / length)
    cosine = jnp.cos(phases)
    sine = jnp.sin(phases)
    forward = jnp.stack([jnp.stack([cosine, sine], 1), jnp.stack([-sine, cosine], 1)], 1)
    inverse = jnp.stack([jnp.stack([cosine, -sine], 1), jnp.stack([sine, cosine], 1)], 1) / length
    frequency = (points - length * (points >= length // 2).astype(jnp.int32)).astype(jnp.float32)
    return forward.astype(jnp.bfloat16), inverse.astype(jnp.bfloat16), frequency


def product(form, left, right):
    return jnp.einsum(form, left.astype(jnp.float32), right.astype(jnp.float32), precision=lax.Precision.HIGHEST)


def apply_ramp(spectrum, phases):
    real_part = spectrum[:, :, 0]
    imag_part = spectrum[:, :, 1]
    cosine = jnp.cos(phases)
    sine = jnp.sin(phases)
    return jnp.stack([real_part * cosine + imag_part * sine, imag_part * cosine - real_part * sine], 2).astype(jnp.bfloat16)


def shear_x(volume, shifts, tables):
    forward, inverse, frequency = tables
    length = volume.shape[3]
    spectrum = product("kpqn,bzqny->bzpky", forward, volume)
    phases = (2.0 * math.pi / length) * shifts[:, :, None, None] * frequency[None, None, :, None]
    ramped = apply_ramp(spectrum, phases)
    return product("npqk,bzqky->bzpny", inverse, ramped).astype(jnp.bfloat16)


def shear_z(volume, shifts, tables):
    forward, inverse, frequency = tables
    length = volume.shape[1]
    spectrum = product("kpqn,bnqxy->bkpxy", forward, volume)
    phases = (2.0 * math.pi / length) * frequency[None, :, None, None] * shifts[:, None, :, None]
    ramped = apply_ramp(spectrum, phases)
    return product("npqk,bkqxy->bnpxy", inverse, ramped).astype(jnp.bfloat16)


def reference(state_images, rot_index, counts):
    tables_x = dft_tables(NX)
    tables_z = dft_tables(NZ)
    z_offsets = jnp.arange(NZ, dtype=jnp.float32) - (NZ - 1) / 2.0
    x_offsets = jnp.arange(NX, dtype=jnp.float32) - (NX - 1) / 2.0

    def accumulate(running, inputs):
        state_image, angle_index, count_value = inputs
        angle = -(angle_index.astype(jnp.float32) - ANGLES // 2) * angle_step
        tilt_shift = jnp.broadcast_to((-jnp.tan(angle / 2.0) * z_offsets)[None, :], (COEF, NZ))
        lift_shift = jnp.broadcast_to((jnp.sin(angle) * x_offsets)[None, :], (COEF, NX))
        first = shear_x(state_image, tilt_shift, tables_x)
        second = shear_z(first, lift_shift, tables_z)
        third = shear_x(second, tilt_shift, tables_x)
        weighted = (third.astype(jnp.float32) * (count_value.astype(jnp.float32) * count_scale)).astype(jnp.bfloat16)
        weighted = lax.optimization_barrier(weighted)
        return running + weighted.astype(jnp.float32), None

    running = jnp.zeros((COEF, NZ, 2, NX, NY), jnp.float32)
    combined, _ = lax.scan(accumulate, running, (state_images, rot_index, counts))
    return combined
```

```python
import math

import jax
import jax.numpy as jnp
import numpy as np
from jax import lax
from jax.experimental import pallas as pl
from jax.experimental.pallas import tpu as pltpu
from jax.sharding import PartitionSpec as P

N = 320
HALF = N // 2
ANGLES = 32
LANES = 640
PAD = 384
WIDE = 2 * PAD
BLOCK = 80
CHUNKS = 4
PACKED = 112
MESH = pl.DeviceIdType.MESH
f32 = jnp.float32
bf16 = jnp.bfloat16


def packed_lane(part, x):
    return np.where(x < 256, part * 256 + x, 512 + part * 64 + (x - 256))


def host_tables():
    points = np.arange(N)
    phase = (points[:, None] * points[None, :] % N) * (2.0 * math.pi / N)
    cosine = np.cos(phase)
    sine = np.sin(phase)
    forward = np.zeros((2, N, 2, PAD))
    forward[0, :, 0, :N] = cosine
    forward[1, :, 0, :N] = sine
    forward[0, :, 1, :N] = -sine
    forward[1, :, 1, :N] = cosine
    forward = forward.reshape(2 * N, WIDE)
    inverse = np.zeros((2, PAD, 2, N))
    inverse[0, :N, 0] = cosine / N
    inverse[1, :N, 0] = -sine / N
    inverse[0, :N, 1] = sine / N
    inverse[1, :N, 1] = cosine / N
    inverse = inverse.reshape(WIDE, 2 * N)
    order = np.zeros(2 * N, np.int64)
    for part in range(2):
        order[packed_lane(part, points)] = part * N + points
    angle = -(np.arange(ANGLES) - ANGLES // 2) * math.pi / 120.0
    shifts = np.stack([-np.tan(angle / 2.0), np.sin(angle)])
    return (
        jnp.asarray(forward.astype(jnp.bfloat16)),
        jnp.asarray(inverse[:, order].astype(jnp.bfloat16)),
        jnp.asarray(forward[order].astype(jnp.bfloat16)),
        jnp.asarray(np.concatenate([cosine, sine]).astype(jnp.bfloat16)),
        jnp.asarray((np.concatenate([cosine, sine]) / N).astype(jnp.bfloat16)),
        jnp.asarray(shifts.astype(np.float32)),
    )


def turn(turns):
    half = (turns - jnp.floor(turns + 0.5)) * math.pi
    sq = half * half
    s = -1.0 / 39916800.0
    for c in (1.0 / 362880.0, -1.0 / 5040.0, 1.0 / 120.0, -1.0 / 6.0, 1.0):
        s = s * sq + c
    s = s * half
    c = 1.0 / 479001600.0
    for k in (-1.0 / 3628800.0, 1.0 / 40320.0, -1.0 / 720.0, 1.0 / 24.0, -0.5, 1.0):
        c = c * sq + k
    return 1.0 - 2.0 * s * s, 2.0 * s * c


def centred(index):
    return jnp.where(index >= HALF, index - N, index).astype(f32)


def kernel(
    rot, counts, shifts, image, fwd_hbm, inv_hbm, fwd3_hbm, fz_hbm, gz_hbm,
    out,
    v, fwd, inv, fwd3, fz, gz,
    cos_x, sin_x, cos_z, sin_z,
    xsend, xrecv, zsend, planes, rsend, rrecv, fsend, frecv,
    turned, second, total, packed, final,
    load_sem, local_sem, xs_sem, xr_sem, zs_sem, zr_sem, ys_sem, yr_sem, fs_sem, fr_sem,
):
    state = lax.axis_index("state")
    slab = lax.axis_index("slab")
    zlo = state // 4
    y = state % 4
    zhi = slab // 8
    x = (slab % 8) // 2
    core = slab % 2
    me = slab % 8

    loads = []
    for i, (src, dst) in enumerate(
        ((image, v), (fwd_hbm, fwd), (inv_hbm, inv), (fz_hbm, fz), (gz_hbm, gz), (fwd3_hbm, fwd3))
    ):
        copy = pltpu.make_async_copy(src, dst, load_sem.at[i])
        copy.start()
        loads.append(copy)

    barrier = pltpu.get_barrier_semaphore()

    def greet(i, _):
        at = lax.rem(zlo * 32 + slab + i, 64)
        pl.semaphore_signal(
            barrier, inc=1,
            device_id={"state": (at // 32) * 4 + y, "slab": lax.rem(at, 32)},
            device_id_type=MESH,
        )
        return 0

    lax.fori_loop(1, 64, greet, 0)
    for i in range(1, 4):
        pl.semaphore_signal(
            barrier, inc=1,
            device_id={"state": zlo * 4 + lax.rem(y + i, 4), "slab": slab},
            device_id_type=MESH,
        )

    tilt = shifts[0, rot[0]]
    lift = shifts[1, rot[0]]
    weight = counts[0].astype(f32) * (1.0 / 64.0)
    centre = (N - 1) / 2.0

    for copy in loads[:3]:
        copy.wait()

    row_freq = centred(lax.broadcasted_iota(jnp.int32, (8, PAD), 1)) * (1.0 / N)

    def first(pair, _):
        blocks = [v[coef, 2 * pair + i] for coef in range(2) for i in range(2)]
        left = jnp.concatenate(blocks, axis=1)
        spectrum = lax.dot_general(left, fwd[...], (((0,), (0,)), ((), ())), preferred_element_type=f32)
        ramped = []
        for b in range(4):
            shift = tilt * ((slab * 10 + 2 * pair + b % 2).astype(f32) - centre)
            cosine, sine = turn(row_freq * shift)
            cosine = jnp.broadcast_to(cosine[0:1], (128, PAD))
            sine = jnp.broadcast_to(sine[0:1], (128, PAD))
            re = spectrum[128 * b : 128 * (b + 1), :PAD]
            im = spectrum[128 * b : 128 * (b + 1), PAD:]
            ramped.append(
                jnp.concatenate([re * cosine + im * sine, im * cosine - re * sine], axis=1).astype(bf16)
            )
        moved = jnp.dot(jnp.concatenate(ramped, axis=0), inv[...], preferred_element_type=f32)
        at = pl.ds(pl.multiple_of(pair * 16, 16), 16)
        for coef in range(2):
            for low in range(2):
                for yy in range(4):
                    for h in range(2):
                        q = low * 64 + yy * 16 + h * 8
                        piece = jnp.concatenate(
                            [moved[256 * coef + q : 256 * coef + q + 8],
                             moved[256 * coef + 128 + q : 256 * coef + 128 + q + 8]], axis=0)
                        xsend[(low * 2 + h) * 2 + coef, yy, at, :] = piece.astype(bf16)
        return 0

    lax.fori_loop(0, 5, first, 0)

    pl.semaphore_wait(barrier, 66)

    def chunk_y(t):
        return lax.rem(y + 1 + t, 4)

    def x_copies(t):
        yy = chunk_y(t)
        out_copies = []
        for o in range(1, 8):
            gx = lax.rem(x + o // 2, 4)
            gc = lax.rem(core + o, 2)
            out_copies.append(pltpu.make_async_remote_copy(
                src_ref=xsend.at[gx * 2 + gc, yy], dst_ref=xrecv.at[t, me],
                send_sem=xs_sem.at[t, o - 1], recv_sem=xr_sem.at[t, o - 1],
                device_id={"slab": zhi * 8 + gx * 2 + gc}, device_id_type=MESH))
        own = pltpu.make_async_copy(xsend.at[me, yy], xrecv.at[t, me], local_sem.at[t])
        return out_copies, own

    def z_copies(t):
        out_copies = []
        for o in range(1, 4):
            gz_at = lax.rem(zhi + o, 4)
            out_copies.append(pltpu.make_async_remote_copy(
                src_ref=zsend.at[t, gz_at],
                dst_ref=planes.at[t, :, pl.ds(pl.multiple_of(zhi * BLOCK, 16), BLOCK), :],
                send_sem=zs_sem.at[t, o - 1], recv_sem=zr_sem.at[t, o - 1],
                device_id={"slab": gz_at * 8 + me}, device_id_type=MESH))
        own = pltpu.make_async_copy(
            zsend.at[t, zhi], planes.at[t, :, pl.ds(pl.multiple_of(zhi * BLOCK, 16), BLOCK), :],
            local_sem.at[CHUNKS + t])
        return out_copies, own

    def y_copy(t):
        return pltpu.make_async_remote_copy(
            src_ref=rsend.at[t], dst_ref=rrecv.at[t],
            send_sem=ys_sem.at[t], recv_sem=yr_sem.at[t],
            device_id={"state": zlo * 4 + chunk_y(t)}, device_id_type=MESH)

    def start(copies):
        remote, own = copies
        for copy in remote:
            copy.start()
        own.start()

    def arrive(copies):
        remote, own = copies
        own.wait()
        for copy in remote:
            copy.wait_recv()

    xc = [x_copies(t) for t in range(CHUNKS)]
    zc = [z_copies(t) for t in range(CHUNKS)]
    yc = [y_copy(t) for t in range(CHUNKS - 1)]
    start(xc[0])

    def tables(i, _):
        rows = pl.ds(pl.multiple_of(i * 16, 16), 16)
        row = lax.broadcasted_iota(jnp.int32, (16, PAD), 0) + i * 16
        lane = lax.broadcasted_iota(jnp.int32, (16, PAD), 1)
        cosine, sine = turn(centred(lane) * (tilt * (row.astype(f32) - centre)) * (1.0 / N))
        cos_x[rows, :] = cosine
        sin_x[rows, :] = sine
        at = jnp.where(lane >= N, lane - 64, lane)
        cosine, sine = turn(centred(row) * (lift * (at.astype(f32) - centre)) * (1.0 / N))
        cos_z[rows, :] = cosine
        sin_z[rows, :] = sine
        return 0

    lax.fori_loop(0, N // 16, tables, 0)
    for copy in loads[3:]:
        copy.wait()

    def transpose(t):
        for lane in range(5):
            for g in range(8):
                turned[lane, BLOCK * g : BLOCK * (g + 1), :] = xrecv[
                    t, g, :, 128 * lane : 128 * (lane + 1)].astype(f32)
        for lane in range(5):
            for m in range(8):
                zsend[t, m // 2, m % 2, :, 128 * lane : 128 * (lane + 1)] = turned[
                    lane, pl.ds(m, BLOCK, stride=8), :].astype(bf16)

    lane128 = lax.broadcasted_iota(jnp.int32, (N, 128), 1)

    def swap(left, right, paired):
        if paired:
            return right, -left
        l = pltpu.roll(left, 64, 1)
        r = pltpu.roll(right, 64, 1)
        return jnp.where(lane128 < 64, l, -l), jnp.where(lane128 < 64, r, -r)

    def shear_planes(t):
        units = [((e, j), (e, 2 + j), j) for e in range(2) for j in range(2)] + [((0, 4), (1, 4), 2)]
        for (ea, ta), (eb, tb), tile in units:
            data = jnp.concatenate(
                [planes[t, ea, :, 128 * ta : 128 * (ta + 1)], planes[t, eb, :, 128 * tb : 128 * (tb + 1)]], axis=1)
            both = jnp.dot(fz[...], data, preferred_element_type=f32)
            cosine = cos_z[:, 128 * tile : 128 * (tile + 1)]
            sine = sin_z[:, 128 * tile : 128 * (tile + 1)]
            near, far = [], []
            for s in range(2):
                tc = both[:N, 128 * s : 128 * (s + 1)]
                ts = both[N:, 128 * s : 128 * (s + 1)]
                near.append(cosine * tc - sine * ts)
                far.append(cosine * ts + sine * tc)
            far = swap(far[0], far[1], tile < 2)
            ramped = jnp.concatenate([near[0] + far[0], near[1] + far[1]], axis=1).astype(bf16)
            both = jnp.dot(gz[...], ramped, preferred_element_type=f32)
            far = swap(both[N:, :128], both[N:, 128:], tile < 2)
            second[ea, :, 128 * ta : 128 * (ta + 1)] = (both[:N, :128] - far[0]).astype(bf16)
            second[eb, :, 128 * tb : 128 * (tb + 1)] = (both[:N, 128:] - far[1]).astype(bf16)
        for e in range(2):
            spectrum = jnp.dot(second[e], fwd3[...], preferred_element_type=f32)
            re, im = spectrum[:, :PAD], spectrum[:, PAD:]
            cosine, sine = cos_x[...], sin_x[...]
            ramped = jnp.concatenate([re * cosine + im * sine, im * cosine - re * sine], axis=1).astype(bf16)
            rsend[t, e] = (jnp.dot(ramped, inv[...], preferred_element_type=f32) * weight).astype(bf16)

    for t in range(CHUNKS):
        arrive(xc[t])
        if t + 1 < CHUNKS:
            start(xc[t + 1])
        transpose(t)
        start(zc[t])
        if t >= 1:
            arrive(zc[t - 1])
            shear_planes(t - 1)
            yc[t - 1].start()
    arrive(zc[CHUNKS - 1])
    shear_planes(CHUNKS - 1)
    for copy in yc:
        copy.wait_recv()

    def add(i, _):
        rows = pl.ds(pl.multiple_of(i * 16, 16), 16)
        for e in range(2):
            acc = rsend[CHUNKS - 1, e, rows, :].astype(f32)
            for t in range(CHUNKS - 1):
                acc = acc + rrecv[t, e, rows, :].astype(f32)
            total[e, rows, :] = acc
        return 0

    lax.fori_loop(0, N // 16, add, 0)

    target = (x // 2) * 4 + y
    slot = ((zlo * 2 + x % 2) * 4 + zhi) * 2 + core

    packed[100:PACKED, :] = jnp.zeros((PACKED - 100, 128), f32)

    def pack(q, _):
        for i in range(4):
            for e in range(2):
                for b in range(5):
                    rows = total[e, pl.ds(pl.multiple_of(q * 40, 8), 40), 128 * b : 128 * (b + 1)]
                    at = (e * 5 + b) * 10
                    packed[at : at + 10, :] = rows[10 * i : 10 * i + 10]
            fsend[q * 4 + i] = packed[...].astype(bf16)
        return 0

    lax.fori_loop(0, 8, pack, 0)

    def f_copy(o):
        to = lax.rem(slab + o, 32)
        return pltpu.make_async_remote_copy(
            src_ref=fsend.at[to], dst_ref=frecv.at[slot],
            send_sem=fs_sem.at[o], recv_sem=fr_sem.at[slot],
            device_id={"state": target, "slab": to}, device_id_type=MESH)

    def f_own():
        return pltpu.make_async_copy(fsend.at[slab], frecv.at[slot], fr_sem.at[slot])

    for o in range(1, 32):
        f_copy(o).start()

    @pl.when(target == state)
    def _():
        f_own().start()

    @pl.when(target != state)
    def _():
        f_copy(0).start()

    for t in range(CHUNKS):
        for copy in xc[t][0] + zc[t][0]:
            copy.wait_send()
    for copy in yc:
        copy.wait_send()

    def land(i, _):
        pltpu.make_async_copy(fsend.at[0], frecv.at[i], fr_sem.at[i]).wait()
        return 0

    lax.fori_loop(0, 32, land, 0)

    for h in range(2):
        for zz in range(4):
            for coef in range(2):
                at = (h * 4 + zz) * 2 + coef
                packed[...] = frecv[at].astype(f32) + frecv[16 + at].astype(f32)
                for e in range(2):
                    row = 8 * h + 2 * zz + e
                    for b in range(5):
                        piece = packed[(e * 5 + b) * 10 : (e * 5 + b) * 10 + 10, :]
                        base = coef * N + row
                        if b < 4:
                            final[b % 2, pl.ds(base + 16 * (b // 2), 10, stride=32), :] = piece
                        else:
                            final[2, pl.ds(base, 10, stride=32), :] = piece
                            final[2, pl.ds(base + 16, 10, stride=32), :] = pltpu.roll(piece, 64, 1)
    out[:, 0:128] = final[0]
    out[:, 128:256] = final[1]
    out[:, 256:320] = final[2][:, :64]

    for o in range(1, 32):
        f_copy(o).wait_send()

    @pl.when(target != state)
    def _():
        f_copy(0).wait_send()


def body(state_images, rot_index, counts):
    fwd, inv, fwd3, fz, gz, shifts = host_tables()
    image = state_images.reshape(2, 10, 2 * N, 128)
    smem = pl.BlockSpec(memory_space=pltpu.SMEM)
    anywhere = pl.BlockSpec(memory_space=pl.ANY)
    dma = pltpu.SemaphoreType.DMA
    vmem = pltpu.VMEM
    out = pl.pallas_call(
        kernel,
        name="shears",
        out_shape=jax.ShapeDtypeStruct((640, N), f32),
        in_specs=[smem, smem, smem] + [anywhere] * 6,
        out_specs=pl.BlockSpec(memory_space=vmem),
        scratch_shapes=[
            vmem(image.shape, bf16), vmem(fwd.shape, bf16), vmem(inv.shape, bf16),
            vmem(fwd3.shape, bf16), vmem(fz.shape, bf16), vmem(gz.shape, bf16),
            vmem((N, PAD), f32), vmem((N, PAD), f32), vmem((N, PAD), f32), vmem((N, PAD), f32),
            vmem((8, 4, BLOCK, LANES), bf16),
            vmem((CHUNKS, 8, BLOCK, LANES), bf16),
            vmem((CHUNKS, 4, 2, BLOCK, LANES), bf16),
            vmem((CHUNKS, 2, N, LANES), bf16),
            vmem((CHUNKS, 2, N, LANES), bf16),
            vmem((CHUNKS - 1, 2, N, LANES), bf16),
            vmem((32, PACKED, 128), bf16),
            vmem((32, PACKED, 128), bf16),
            vmem((5, 640, 128), f32),
            vmem((2, N, LANES), bf16),
            vmem((2, N, LANES), f32),
            vmem((PACKED, 128), f32),
            vmem((3, 640, 128), f32),
            dma((6,)), dma((2 * CHUNKS,)),
            dma((CHUNKS, 7)), dma((CHUNKS, 7)),
            dma((CHUNKS, 3)), dma((CHUNKS, 3)),
            dma((CHUNKS - 1,)), dma((CHUNKS - 1,)),
            dma((32,)), dma((32,)),
        ],
        compiler_params=pltpu.CompilerParams(
            collective_id=0, has_side_effects=True, vmem_limit_bytes=60 * 1024 * 1024),
        cost_estimate=pl.CostEstimate(flops=13_000_000_000, bytes_accessed=8_000_000, transcendentals=0),
    )(rot_index, counts, shifts, image, fwd, inv, fwd3, fz, gz)
    return out.reshape(2, 10, 2, 16, N).swapaxes(3, 4)


def solution(mesh):
    placed = (P("state", None, "slab", None, None, None), P("state"), P("state"))
    return jax.shard_map(
        body,
        mesh=mesh,
        in_specs=placed,
        out_specs=P(None, "slab", None, None, "state"),
        check_vma=False,
    )
```

```python
import math

import jax
import jax.numpy as jnp
import numpy as np
from jax import lax
from jax.experimental import pallas as pl
from jax.experimental.pallas import tpu as pltpu
from jax.sharding import PartitionSpec as P

N = 320
HALF = N // 2
ANGLES = 32
LANES = 640
PAD = 384
WIDE = 2 * PAD
BLOCK = 80
CHUNKS = 4
PACKED = 64
FILLED = 50
RING = 8
MESH = pl.DeviceIdType.MESH
f32 = jnp.float32
bf16 = jnp.bfloat16


def packed_lane(part, x):
    return np.where(x < 256, x // 128 * 256 + part * 128 + x % 128, 512 + part * 64 + (x - 256))


def host_tables():
    points = np.arange(N)
    phase = (points[:, None] * points[None, :] % N) * (2.0 * math.pi / N)
    cosine = np.cos(phase)
    sine = np.sin(phase)
    forward = np.zeros((2, N, 2, PAD))
    forward[0, :, 0, :N] = cosine
    forward[1, :, 0, :N] = sine
    forward[0, :, 1, :N] = -sine
    forward[1, :, 1, :N] = cosine
    forward = forward.reshape(2 * N, WIDE)
    inverse = np.zeros((2, PAD, 2, N))
    inverse[0, :N, 0] = cosine / N
    inverse[1, :N, 0] = -sine / N
    inverse[0, :N, 1] = sine / N
    inverse[1, :N, 1] = cosine / N
    inverse = inverse.reshape(WIDE, 2 * N)
    order = np.zeros(2 * N, np.int64)
    for part in range(2):
        order[packed_lane(part, points)] = part * N + points
    angle = -(np.arange(ANGLES) - ANGLES // 2) * math.pi / 120.0
    shifts = np.stack([-np.tan(angle / 2.0), np.sin(angle)])
    return (
        jnp.asarray(forward.astype(jnp.bfloat16)),
        jnp.asarray(inverse[:, order].astype(jnp.bfloat16)),
        jnp.asarray(forward[order].astype(jnp.bfloat16)),
        jnp.asarray(np.concatenate([cosine, sine]).astype(jnp.bfloat16)),
        jnp.asarray((np.concatenate([cosine, sine]) / N).astype(jnp.bfloat16)),
        jnp.asarray(shifts.astype(np.float32)),
    )


def turn(turns):
    half = (turns - jnp.floor(turns + 0.5)) * math.pi
    sq = half * half
    s = -1.0 / 39916800.0
    for c in (1.0 / 362880.0, -1.0 / 5040.0, 1.0 / 120.0, -1.0 / 6.0, 1.0):
        s = s * sq + c
    s = s * half
    c = 1.0 / 479001600.0
    for k in (-1.0 / 3628800.0, 1.0 / 40320.0, -1.0 / 720.0, 1.0 / 24.0, -0.5, 1.0):
        c = c * sq + k
    return 1.0 - 2.0 * s * s, 2.0 * s * c


def centred(index):
    return jnp.where(index >= HALF, index - N, index).astype(f32)


def kernel(
    rot, counts, shifts, image, fwd_hbm, inv_hbm, fwd3_hbm, fz_hbm, gz_hbm,
    out,
    v, fwd, inv, fwd3, fz, gz,
    cos_x, sin_x, cos_z, sin_z,
    xsend, xrecv, zsend, planes, rsend, rrecv, fsend, frecv,
    params, turned, second, total, packed, final,
    load_sem, local_sem, ps_sem, pr_sem, xs_sem, xr_sem, zs_sem, zr_sem, ys_sem, yr_sem, fs_sem, fr_sem,
):
    state = lax.axis_index("state")
    slab = lax.axis_index("slab")
    zlo = state // 4
    y = state % 4
    zhi = slab // 8
    x = (slab % 8) // 2
    core = slab % 2
    me = slab % 8
    spot = zhi * 2 + zlo

    loads = []
    for i, (src, dst) in enumerate(
        ((image, v), (fwd_hbm, fwd), (inv_hbm, inv), (fz_hbm, fz), (gz_hbm, gz), (fwd3_hbm, fwd3))
    ):
        copy = pltpu.make_async_copy(src, dst, load_sem.at[i])
        copy.start()
        loads.append(copy)

    barrier = pltpu.get_barrier_semaphore()

    def greet(i, _):
        at = lax.rem(zlo * 32 + slab + i, 64)
        pl.semaphore_signal(
            barrier, inc=1,
            device_id={"state": (at // 32) * 4 + y, "slab": lax.rem(at, 32)},
            device_id_type=MESH,
        )
        return 0

    lax.fori_loop(1, 64, greet, 0)
    for i in range(1, 4):
        pl.semaphore_signal(
            barrier, inc=1,
            device_id={"state": zlo * 4 + lax.rem(y + i, 4), "slab": slab},
            device_id_type=MESH,
        )

    tilt = shifts[0, rot[0]]
    lift = shifts[1, rot[0]]
    weight = counts[0].astype(f32) * (1.0 / 64.0)
    centre = (N - 1) / 2.0

    for copy in loads[:3]:
        copy.wait()

    row_freq = centred(lax.broadcasted_iota(jnp.int32, (8, PAD), 1)) * (1.0 / N)

    def first(pair, _):
        blocks = [v[coef, 2 * pair + i] for coef in range(2) for i in range(2)]
        left = jnp.concatenate(blocks, axis=1)
        spectrum = lax.dot_general(left, fwd[...], (((0,), (0,)), ((), ())), preferred_element_type=f32)
        ramped = []
        for b in range(4):
            shift = tilt * ((slab * 10 + 2 * pair + b % 2).astype(f32) - centre)
            cosine, sine = turn(row_freq * shift)
            cosine = jnp.broadcast_to(cosine[0:1], (128, PAD))
            sine = jnp.broadcast_to(sine[0:1], (128, PAD))
            re = spectrum[128 * b : 128 * (b + 1), :PAD]
            im = spectrum[128 * b : 128 * (b + 1), PAD:]
            ramped.append(
                jnp.concatenate([re * cosine + im * sine, im * cosine - re * sine], axis=1).astype(bf16)
            )
        moved = jnp.dot(jnp.concatenate(ramped, axis=0), inv[...], preferred_element_type=f32)
        at = pl.ds(pl.multiple_of(pair * 16, 16), 16)
        for coef in range(2):
            for low in range(2):
                for yy in range(4):
                    for h in range(2):
                        q = low * 64 + yy * 16 + h * 8
                        piece = jnp.concatenate(
                            [moved[256 * coef + q : 256 * coef + q + 8],
                             moved[256 * coef + 128 + q : 256 * coef + 128 + q + 8]], axis=0)
                        xsend[(coef * 2 + h) * 2 + low, yy, at, :] = piece.astype(bf16)
        return 0

    lax.fori_loop(0, 5, first, 0)

    pl.semaphore_wait(barrier, 66)

    def chunk_y(t):
        return lax.rem(y + 1 + t, 4)

    def x_copies(t):
        yy = chunk_y(t)
        out_copies = []
        for o in range(1, 8):
            gx = lax.rem(x + o // 2, 4)
            gc = lax.rem(core + o, 2)
            out_copies.append(pltpu.make_async_remote_copy(
                src_ref=xsend.at[gx * 2 + gc, yy], dst_ref=xrecv.at[t, me],
                send_sem=xs_sem.at[t, o - 1], recv_sem=xr_sem.at[t, o - 1],
                device_id={"slab": zhi * 8 + gx * 2 + gc}, device_id_type=MESH))
        own = pltpu.make_async_copy(xsend.at[me, yy], xrecv.at[t, me], local_sem.at[t])
        return out_copies, own

    def z_copies(t):
        out_copies = []
        dst = planes.at[t, zlo, pl.ds(pl.multiple_of(zhi * BLOCK, 16), BLOCK), :]
        for o in range(1, RING):
            to = lax.rem(spot + o, RING)
            out_copies.append(pltpu.make_async_remote_copy(
                src_ref=zsend.at[t, to], dst_ref=dst,
                send_sem=zs_sem.at[t, o - 1], recv_sem=zr_sem.at[t, o - 1],
                device_id={"state": (to % 2) * 4 + y, "slab": (to // 2) * 8 + me}, device_id_type=MESH))
        own = pltpu.make_async_copy(zsend.at[t, spot], dst, local_sem.at[CHUNKS + t])
        return out_copies, own

    def y_copy(t):
        return pltpu.make_async_remote_copy(
            src_ref=rsend.at[t], dst_ref=rrecv.at[t],
            send_sem=ys_sem.at[t], recv_sem=yr_sem.at[t],
            device_id={"state": zlo * 4 + chunk_y(t)}, device_id_type=MESH)

    def start(copies):
        remote, own = copies
        for copy in remote:
            copy.start()
        own.start()

    def arrive(copies):
        remote, own = copies
        own.wait()
        for copy in remote:
            copy.wait_recv()

    xc = [x_copies(t) for t in range(CHUNKS)]
    zc = [z_copies(t) for t in range(CHUNKS)]
    yc = [y_copy(t) for t in range(CHUNKS - 1)]
    start(xc[0])

    row8 = lax.broadcasted_iota(jnp.int32, (8, 128), 0)
    params[zlo] = jnp.where(row8 == 0, tilt, jnp.where(row8 == 1, lift, weight))
    swap_params = pltpu.make_async_remote_copy(
        src_ref=params.at[zlo], dst_ref=params.at[zlo], send_sem=ps_sem, recv_sem=pr_sem,
        device_id={"state": (1 - zlo) * 4 + y}, device_id_type=MESH)
    swap_params.start()
    swap_params.wait()

    def tables(i, _):
        row = (lax.broadcasted_iota(jnp.int32, (16, 128), 0) + i * 16)
        for s in range(2):
            rows = pl.ds(pl.multiple_of(s * N + i * 16, 16), 16)
            tilt_s = params[s, 0:1, :]
            lift_s = params[s, 1:2, :]
            for tile in range(3):
                lanes = slice(128 * tile, 128 * (tile + 1))
                lane = lax.broadcasted_iota(jnp.int32, (16, 128), 1) + 128 * tile
                cosine, sine = turn(centred(lane) * (tilt_s * (row.astype(f32) - centre)) * (1.0 / N))
                cos_x[rows, lanes] = cosine
                sin_x[rows, lanes] = sine
                at = jnp.where(lane >= N, lane - 64, lane)
                cosine, sine = turn(centred(row) * (lift_s * (at.astype(f32) - centre)) * (1.0 / N))
                cos_z[rows, lanes] = cosine
                sin_z[rows, lanes] = sine
        return 0

    lax.fori_loop(0, N // 16, tables, 0)
    for copy in loads[3:]:
        copy.wait()

    def transpose(t):
        for lane in range(5):
            for g in range(8):
                turned[lane, BLOCK * g : BLOCK * (g + 1), :] = xrecv[
                    t, g, :, 128 * lane : 128 * (lane + 1)].astype(f32)
        for lane in range(5):
            for m in range(8):
                zsend[t, m, :, 128 * lane : 128 * (lane + 1)] = turned[
                    lane, pl.ds(m, BLOCK, stride=8), :].astype(bf16)

    lane128 = lax.broadcasted_iota(jnp.int32, (N, 128), 1)

    def swap(left, right, paired):
        if paired:
            return right, -left
        l = pltpu.roll(left, 64, 1)
        r = pltpu.roll(right, 64, 1)
        return jnp.where(lane128 < 64, l, -l), jnp.where(lane128 < 64, r, -r)

    def shear_planes(t):
        units = [((s, 2 * u), (s, 2 * u + 1), u) for u in range(2) for s in range(2)] + [((0, 4), (1, 4), 2)]
        for sides in units:
            tile = sides[2]
            pair = sides[:2]
            data = jnp.concatenate([planes[t, s, :, 128 * b : 128 * (b + 1)] for s, b in pair], axis=1)
            both = jnp.dot(fz[...], data, preferred_element_type=f32)
            near, far = [], []
            for i, (s, b) in enumerate(pair):
                cosine = cos_z[s * N : (s + 1) * N, 128 * tile : 128 * (tile + 1)]
                sine = sin_z[s * N : (s + 1) * N, 128 * tile : 128 * (tile + 1)]
                tc = both[:N, 128 * i : 128 * (i + 1)]
                ts = both[N:, 128 * i : 128 * (i + 1)]
                near.append(cosine * tc - sine * ts)
                far.append(cosine * ts + sine * tc)
            far = swap(far[0], far[1], tile < 2)
            ramped = jnp.concatenate([near[0] + far[0], near[1] + far[1]], axis=1).astype(bf16)
            both = jnp.dot(gz[...], ramped, preferred_element_type=f32)
            far = swap(both[N:, :128], both[N:, 128:], tile < 2)
            for i, (s, b) in enumerate(pair):
                second[s * N : (s + 1) * N, 128 * b : 128 * (b + 1)] = (
                    both[:N, 128 * i : 128 * (i + 1)] - far[i]).astype(bf16)
        spectrum = jnp.dot(second[...], fwd3[...], preferred_element_type=f32)
        re, im = spectrum[:, :PAD], spectrum[:, PAD:]
        cosine, sine = cos_x[...], sin_x[...]
        ramped = jnp.concatenate([re * cosine + im * sine, im * cosine - re * sine], axis=1).astype(bf16)
        moved = jnp.dot(ramped, inv[...], preferred_element_type=f32)
        w0 = jnp.concatenate([params[0, 2:3, :]] * 5, axis=1)
        w1 = jnp.concatenate([params[1, 2:3, :]] * 5, axis=1)
        rsend[t] = (moved[:N] * w0 + moved[N:] * w1).astype(bf16)

    for t in range(CHUNKS):
        arrive(xc[t])
        if t + 1 < CHUNKS:
            start(xc[t + 1])
        transpose(t)
        start(zc[t])
        if t >= 1:
            arrive(zc[t - 1])
            shear_planes(t - 1)
            yc[t - 1].start()
    arrive(zc[CHUNKS - 1])
    shear_planes(CHUNKS - 1)
    for copy in yc:
        copy.wait_recv()

    def add(i, _):
        rows = pl.ds(pl.multiple_of(i * 16, 16), 16)
        acc = rsend[CHUNKS - 1, rows, :].astype(f32)
        for t in range(CHUNKS - 1):
            acc = acc + rrecv[t, rows, :].astype(f32)
        total[rows, :] = acc
        return 0

    lax.fori_loop(0, N // 16, add, 0)

    target = core * 4 + y
    slot = x * RING + spot

    packed[FILLED:PACKED, :] = jnp.zeros((PACKED - FILLED, 128), f32)

    def pack(q, _):
        for i in range(4):
            for b in range(5):
                rows = total[pl.ds(pl.multiple_of(q * 40, 8), 40), 128 * b : 128 * (b + 1)]
                packed[b * 10 : b * 10 + 10, :] = rows[10 * i : 10 * i + 10]
            fsend[q * 4 + i] = packed[...].astype(bf16)
        return 0

    lax.fori_loop(0, 8, pack, 0)

    def f_copy(o):
        to = lax.rem(slab + o, 32)
        return pltpu.make_async_remote_copy(
            src_ref=fsend.at[to], dst_ref=frecv.at[slot],
            send_sem=fs_sem.at[o], recv_sem=fr_sem.at[slot],
            device_id={"state": target, "slab": to}, device_id_type=MESH)

    def f_own():
        return pltpu.make_async_copy(fsend.at[slab], frecv.at[slot], fr_sem.at[slot])

    for o in range(1, 32):
        f_copy(o).start()

    @pl.when(target == state)
    def _():
        f_own().start()

    @pl.when(target != state)
    def _():
        f_copy(0).start()

    for t in range(CHUNKS):
        for copy in xc[t][0] + zc[t][0]:
            copy.wait_send()
    for copy in yc:
        copy.wait_send()

    def land(i, _):
        pltpu.make_async_copy(fsend.at[0], frecv.at[i], fr_sem.at[i]).wait()
        return 0

    lax.fori_loop(0, 32, land, 0)

    for coef in range(2):
        for h in range(2):
            for at in range(RING):
                packed[...] = frecv[(coef * 2 + h) * RING + at].astype(f32)
                for b in range(5):
                    piece = packed[b * 10 : b * 10 + 10, :]
                    base = coef * N + 8 * h + at
                    if b < 4:
                        final[b // 2, pl.ds(base + 16 * (b % 2), 10, stride=32), :] = piece
                    else:
                        final[2, pl.ds(base, 10, stride=32), :] = piece
                        final[2, pl.ds(base + 16, 10, stride=32), :] = pltpu.roll(piece, 64, 1)
    out[:, 0:128] = final[0]
    out[:, 128:256] = final[1]
    out[:, 256:320] = final[2][:, :64]

    for o in range(1, 32):
        f_copy(o).wait_send()

    @pl.when(target != state)
    def _():
        f_copy(0).wait_send()


def body(state_images, rot_index, counts):
    fwd, inv, fwd3, fz, gz, shifts = host_tables()
    image = state_images.reshape(2, 10, 2 * N, 128)
    smem = pl.BlockSpec(memory_space=pltpu.SMEM)
    anywhere = pl.BlockSpec(memory_space=pl.ANY)
    dma = pltpu.SemaphoreType.DMA
    vmem = pltpu.VMEM
    out = pl.pallas_call(
        kernel,
        name="shears",
        out_shape=jax.ShapeDtypeStruct((640, N), f32),
        in_specs=[smem, smem, smem] + [anywhere] * 6,
        out_specs=pl.BlockSpec(memory_space=vmem),
        scratch_shapes=[
            vmem(image.shape, bf16), vmem(fwd.shape, bf16), vmem(inv.shape, bf16),
            vmem(fwd3.shape, bf16), vmem(fz.shape, bf16), vmem(gz.shape, bf16),
            vmem((2 * N, PAD), f32), vmem((2 * N, PAD), f32), vmem((2 * N, PAD), f32), vmem((2 * N, PAD), f32),
            vmem((8, 4, BLOCK, LANES), bf16),
            vmem((CHUNKS, 8, BLOCK, LANES), bf16),
            vmem((CHUNKS, RING, BLOCK, LANES), bf16),
            vmem((CHUNKS, 2, N, LANES), bf16),
            vmem((CHUNKS, N, LANES), bf16),
            vmem((CHUNKS - 1, N, LANES), bf16),
            vmem((32, PACKED, 128), bf16),
            vmem((32, PACKED, 128), bf16),
            vmem((2, 8, 128), f32),
            vmem((5, 640, 128), f32),
            vmem((2 * N, LANES), bf16),
            vmem((N, LANES), f32),
            vmem((PACKED, 128), f32),
            vmem((3, 640, 128), f32),
            dma((6,)), dma((2 * CHUNKS,)), dma, dma,
            dma((CHUNKS, 7)), dma((CHUNKS, 7)),
            dma((CHUNKS, RING - 1)), dma((CHUNKS, RING - 1)),
            dma((CHUNKS - 1,)), dma((CHUNKS - 1,)),
            dma((32,)), dma((32,)),
        ],
        compiler_params=pltpu.CompilerParams(
            collective_id=0, has_side_effects=True, vmem_limit_bytes=60 * 1024 * 1024),
        cost_estimate=pl.CostEstimate(flops=13_000_000_000, bytes_accessed=8_000_000, transcendentals=0),
    )(rot_index, counts, shifts, image, fwd, inv, fwd3, fz, gz)
    return out.reshape(2, 10, 2, 16, N).swapaxes(3, 4)


def solution(mesh):
    placed = (P("state", None, "slab", None, None, None), P("state"), P("state"))
    return jax.shard_map(
        body,
        mesh=mesh,
        in_specs=placed,
        out_specs=P(None, "slab", None, None, "state"),
        check_vma=False,
    )
```

```python
import math

import jax
import jax.numpy as jnp
import numpy as np
from jax import lax
from jax.experimental import pallas as pl
from jax.experimental.pallas import tpu as pltpu
from jax.sharding import PartitionSpec as P

N = 320
HALF = N // 2
ANGLES = 32
LANES = 640
PAD = 384
WIDE = 2 * PAD
BLOCK = 80
CHUNKS = 4
PACKED = 64
FILLED = 50
RING = 8
MESH = pl.DeviceIdType.MESH
f32 = jnp.float32
bf16 = jnp.bfloat16


def packed_lane(part, x):
    return np.where(x < 256, x // 128 * 256 + part * 128 + x % 128, 512 + part * 64 + (x - 256))


def host_tables():
    points = np.arange(N)
    phase = (points[:, None] * points[None, :] % N) * (2.0 * math.pi / N)
    cosine = np.cos(phase)
    sine = np.sin(phase)
    forward = np.zeros((2, N, 2, PAD))
    forward[0, :, 0, :N] = cosine
    forward[1, :, 0, :N] = sine
    forward[0, :, 1, :N] = -sine
    forward[1, :, 1, :N] = cosine
    forward = forward.reshape(2 * N, WIDE)
    inverse = np.zeros((2, PAD, 2, N))
    inverse[0, :N, 0] = cosine / N
    inverse[1, :N, 0] = -sine / N
    inverse[0, :N, 1] = sine / N
    inverse[1, :N, 1] = cosine / N
    inverse = inverse.reshape(WIDE, 2 * N)
    order = np.zeros(2 * N, np.int64)
    for part in range(2):
        order[packed_lane(part, points)] = part * N + points
    angle = -(np.arange(ANGLES) - ANGLES // 2) * math.pi / 120.0
    shifts = np.stack([-np.tan(angle / 2.0), np.sin(angle)])
    return (
        jnp.asarray(forward.astype(jnp.bfloat16)),
        jnp.asarray(inverse[:, order].astype(jnp.bfloat16)),
        jnp.asarray(forward[order].astype(jnp.bfloat16)),
        jnp.asarray(np.concatenate([cosine, sine]).astype(jnp.bfloat16)),
        jnp.asarray((np.concatenate([cosine, sine]) / N).astype(jnp.bfloat16)),
        jnp.asarray(shifts.astype(np.float32)),
    )


def turn(turns):
    half = (turns - jnp.floor(turns + 0.5)) * math.pi
    sq = half * half
    s = -1.0 / 39916800.0
    for c in (1.0 / 362880.0, -1.0 / 5040.0, 1.0 / 120.0, -1.0 / 6.0, 1.0):
        s = s * sq + c
    s = s * half
    c = 1.0 / 479001600.0
    for k in (-1.0 / 3628800.0, 1.0 / 40320.0, -1.0 / 720.0, 1.0 / 24.0, -0.5, 1.0):
        c = c * sq + k
    return 1.0 - 2.0 * s * s, 2.0 * s * c


def centred(index):
    return jnp.where(index >= HALF, index - N, index).astype(f32)


def unit_lanes(u):
    return slice(256 * u, 256 * u + (256 if u < 2 else 128))


def kernel(
    rot_hbm, counts_hbm, shifts, image, fwd_hbm, inv_hbm, fwd3_hbm, fz_hbm, gz_hbm,
    out,
    rot, counts, v, vt, fwd, inv, fwd3, fz, gz,
    cos_f, sin_f, cos_x, sin_x, cos_z, sin_z,
    xsend, xrecv, zsend, planes, rsend, rrecv, fsend, frecv,
    params, turned, second, total, packed, final,
    image_sem, load_sem, xl_sem, zl_sem, ps_sem, pr_sem,
    xs_sem, xr_sem, zs_sem, zr_sem, ys_sem, yr_sem, fs_sem, fr_sem,
):
    state = lax.axis_index("state")
    slab = lax.axis_index("slab")
    zlo = state // 4
    y = state % 4
    zhi = slab // 8
    x = (slab % 8) // 2
    core = slab % 2
    me = slab % 8
    spot = zhi * 2 + zlo

    def image_load(i):
        part = pl.ds(2 * i, 2)
        return pltpu.make_async_copy(image.at[:, part], v.at[:, part], image_sem.at[i])

    loads = [
        pltpu.make_async_copy(src, dst, load_sem.at[i])
        for i, (src, dst) in enumerate(
            ((rot_hbm, rot), (counts_hbm, counts), (fwd_hbm, fwd), (inv_hbm, inv),
             (fz_hbm, fz), (gz_hbm, gz), (fwd3_hbm, fwd3))
        )
    ]
    for copy in loads[:2]:
        copy.start()
    for i in range(5):
        image_load(i).start()
    for copy in loads[2:]:
        copy.start()

    barrier = pltpu.get_barrier_semaphore()

    def greet(i, _):
        at = lax.rem(zlo * 32 + slab + i, 64)
        pl.semaphore_signal(
            barrier, inc=1,
            device_id={"state": (at // 32) * 4 + y, "slab": lax.rem(at, 32)},
            device_id_type=MESH,
        )
        return 0

    lax.fori_loop(1, 64, greet, 0)
    for i in range(1, 4):
        pl.semaphore_signal(
            barrier, inc=1,
            device_id={"state": zlo * 4 + lax.rem(y + i, 4), "slab": slab},
            device_id_type=MESH,
        )

    for copy in loads[:2]:
        copy.wait()
    tilt = shifts[0, rot[0]]
    lift = shifts[1, rot[0]]
    weight = counts[0].astype(f32) * (1.0 / 64.0)
    centre = (N - 1) / 2.0

    row = lax.broadcasted_iota(jnp.int32, (16, PAD), 0) + slab * 10
    freq = centred(lax.broadcasted_iota(jnp.int32, (16, PAD), 1)) * (1.0 / N)
    cosine, sine = turn(freq * (tilt * (row.astype(f32) - centre)))
    cos_f[...] = cosine
    sin_f[...] = sine

    row8 = lax.broadcasted_iota(jnp.int32, (8, 128), 0)
    params[zlo] = jnp.where(row8 == 0, tilt, jnp.where(row8 == 1, lift, weight))
    swap_params = pltpu.make_async_remote_copy(
        src_ref=params.at[zlo], dst_ref=params.at[zlo], send_sem=ps_sem, recv_sem=pr_sem,
        device_id={"state": (1 - zlo) * 4 + y}, device_id_type=MESH)

    def turn_image(i, _):
        image_load(i).wait()
        for coef in range(2):
            for j in range(2):
                vt[coef, 2 * i + j] = v[coef, 2 * i + j].T
        return 0

    lax.fori_loop(0, 5, turn_image, 0)
    for copy in loads[2:4]:
        copy.wait()

    def chunk_y(t):
        return lax.rem(y + 1 + t, 4)

    def first(t):
        yy = chunk_y(t)
        left = jnp.concatenate(
            [vt[coef, z, pl.ds(pl.multiple_of(64 * low + 16 * yy, 16), 16), :]
             for z in range(10) for coef in range(2) for low in range(2)], axis=0)
        spectrum = jnp.dot(left, fwd[...], preferred_element_type=f32)
        ramped = []
        for z in range(10):
            cosine = jnp.broadcast_to(cos_f[z : z + 1, :], (64, PAD))
            sine = jnp.broadcast_to(sin_f[z : z + 1, :], (64, PAD))
            re = spectrum[64 * z : 64 * (z + 1), :PAD]
            im = spectrum[64 * z : 64 * (z + 1), PAD:]
            ramped.append(
                jnp.concatenate([re * cosine + im * sine, im * cosine - re * sine], axis=1).astype(bf16))
        moved = jnp.dot(jnp.concatenate(ramped, axis=0), inv[...], preferred_element_type=f32)
        for pair in range(5):
            for coef in range(2):
                for low in range(2):
                    for h in range(2):
                        q = 128 * pair + 32 * coef + 16 * low + 8 * h
                        piece = jnp.concatenate([moved[q : q + 8], moved[q + 64 : q + 72]], axis=0)
                        xsend[(coef * 2 + h) * 2 + low, t, 16 * pair : 16 * (pair + 1), :] = piece.astype(bf16)

    def x_copies(t, u):
        lanes = unit_lanes(u)
        lanes = pl.ds(lanes.start, lanes.stop - lanes.start)
        out_copies = []
        for o in range(1, 8):
            gx = lax.rem(x + o // 2, 4)
            gc = lax.rem(core + o, 2)
            out_copies.append(pltpu.make_async_remote_copy(
                src_ref=xsend.at[gx * 2 + gc, t, :, lanes], dst_ref=xrecv.at[t, me, :, lanes],
                send_sem=xs_sem.at[t, u, o - 1], recv_sem=xr_sem.at[t, u, o - 1],
                device_id={"slab": zhi * 8 + gx * 2 + gc}, device_id_type=MESH))
        own = pltpu.make_async_copy(
            xsend.at[me, t, :, lanes], xrecv.at[t, me, :, lanes], xl_sem.at[t, u])
        return out_copies, own

    def z_copies(t, u):
        lanes = unit_lanes(u)
        lanes = pl.ds(lanes.start, lanes.stop - lanes.start)
        out_copies = []
        dst = planes.at[t, zlo, pl.ds(pl.multiple_of(zhi * BLOCK, 16), BLOCK), lanes]
        for o in (4, 3, 5, 2, 6, 1, 7):
            to = lax.rem(spot + o, RING)
            out_copies.append(pltpu.make_async_remote_copy(
                src_ref=zsend.at[t, to, :, lanes], dst_ref=dst,
                send_sem=zs_sem.at[t, u, o - 1], recv_sem=zr_sem.at[t, u, o - 1],
                device_id={"state": (to % 2) * 4 + y, "slab": (to // 2) * 8 + me}, device_id_type=MESH))
        own = pltpu.make_async_copy(zsend.at[t, spot, :, lanes], dst, zl_sem.at[t, u])
        return out_copies, own

    def y_copy(t):
        return pltpu.make_async_remote_copy(
            src_ref=rsend.at[t], dst_ref=rrecv.at[t],
            send_sem=ys_sem.at[t], recv_sem=yr_sem.at[t],
            device_id={"state": zlo * 4 + chunk_y(t)}, device_id_type=MESH)

    def start(copies):
        remote, own = copies
        for copy in remote:
            copy.start()
        own.start()

    def arrive(copies):
        remote, own = copies
        own.wait()
        for copy in remote:
            copy.wait_recv()

    first(0)
    pl.semaphore_wait(barrier, 66)
    start(x_copies(0, 0))
    swap_params.start()
    start(x_copies(0, 1))
    start(x_copies(0, 2))
    for copy in loads[4:]:
        copy.wait()
    swap_params.wait()

    def tables(i, _):
        row = lax.broadcasted_iota(jnp.int32, (16, 128), 0) + i * 16
        for s in range(2):
            rows = pl.ds(pl.multiple_of(s * N + i * 16, 16), 16)
            tilt_s = params[s, 0:1, :]
            lift_s = params[s, 1:2, :]
            for tile in range(3):
                lanes = slice(128 * tile, 128 * (tile + 1))
                lane = lax.broadcasted_iota(jnp.int32, (16, 128), 1) + 128 * tile
                cosine, sine = turn(centred(lane) * (tilt_s * (row.astype(f32) - centre)) * (1.0 / N))
                cos_x[rows, lanes] = cosine
                sin_x[rows, lanes] = sine
                at = jnp.where(lane >= N, lane - 64, lane)
                cosine, sine = turn(centred(row) * (lift_s * (at.astype(f32) - centre)) * (1.0 / N))
                cos_z[rows, lanes] = cosine
                sin_z[rows, lanes] = sine
        return 0

    def transpose(t, u):
        lanes = unit_lanes(u)
        for lane in range(lanes.start // 128, lanes.stop // 128):
            for g in range(8):
                turned[lane, BLOCK * g : BLOCK * (g + 1), :] = xrecv[
                    t, g, :, 128 * lane : 128 * (lane + 1)].astype(f32)
        for lane in range(lanes.start // 128, lanes.stop // 128):
            for m in range(8):
                zsend[t, m, :, 128 * lane : 128 * (lane + 1)] = turned[
                    lane, pl.ds(m, BLOCK, stride=8), :].astype(bf16)

    lane128 = lax.broadcasted_iota(jnp.int32, (N, 128), 1)

    def swap(left, right, paired):
        if paired:
            return right, -left
        l = pltpu.roll(left, 64, 1)
        r = pltpu.roll(right, 64, 1)
        return jnp.where(lane128 < 64, l, -l), jnp.where(lane128 < 64, r, -r)

    def shear_z(t, u):
        if u < 2:
            pairs = [((s, 2 * u), (s, 2 * u + 1)) for s in range(2)]
        else:
            pairs = [((0, 4), (1, 4))]
        for pair in pairs:
            data = jnp.concatenate([planes[t, s, :, 128 * b : 128 * (b + 1)] for s, b in pair], axis=1)
            both = jnp.dot(fz[...], data, preferred_element_type=f32)
            near, far = [], []
            for i, (s, b) in enumerate(pair):
                cosine = cos_z[s * N : (s + 1) * N, 128 * u : 128 * (u + 1)]
                sine = sin_z[s * N : (s + 1) * N, 128 * u : 128 * (u + 1)]
                tc = both[:N, 128 * i : 128 * (i + 1)]
                ts = both[N:, 128 * i : 128 * (i + 1)]
                near.append(cosine * tc - sine * ts)
                far.append(cosine * ts + sine * tc)
            far = swap(far[0], far[1], u < 2)
            ramped = jnp.concatenate([near[0] + far[0], near[1] + far[1]], axis=1).astype(bf16)
            both = jnp.dot(gz[...], ramped, preferred_element_type=f32)
            far = swap(both[N:, :128], both[N:, 128:], u < 2)
            for i, (s, b) in enumerate(pair):
                second[s * N : (s + 1) * N, 128 * b : 128 * (b + 1)] = (
                    both[:N, 128 * i : 128 * (i + 1)] - far[i]).astype(bf16)

    def shear_x(t):
        spectrum = jnp.dot(second[...], fwd3[...], preferred_element_type=f32)
        re, im = spectrum[:, :PAD], spectrum[:, PAD:]
        cosine, sine = cos_x[...], sin_x[...]
        ramped = jnp.concatenate([re * cosine + im * sine, im * cosine - re * sine], axis=1).astype(bf16)
        moved = jnp.dot(ramped, inv[...], preferred_element_type=f32)
        w0 = jnp.concatenate([params[0, 2:3, :]] * 5, axis=1)
        w1 = jnp.concatenate([params[1, 2:3, :]] * 5, axis=1)
        rsend[t] = (moved[:N] * w0 + moved[N:] * w1).astype(bf16)

    def step(t, _):
        @pl.when(t < CHUNKS - 1)
        def _():
            first(t + 1)

        @pl.when(t < CHUNKS)
        def _():
            for u in range(3):
                arrive(x_copies(t, u))
                transpose(t, u)
                start(z_copies(t, u))

                @pl.when(t < CHUNKS - 1)
                def _():
                    start(x_copies(t + 1, u))

        @pl.when(t == 0)
        def _():
            lax.fori_loop(0, N // 16, tables, 0)

        @pl.when(t >= 1)
        def _():
            for u in range(3):
                arrive(z_copies(t - 1, u))
                shear_z(t - 1, u)
            shear_x(t - 1)

            @pl.when(t < CHUNKS)
            def _():
                y_copy(t - 1).start()

        return 0

    lax.fori_loop(0, CHUNKS + 1, step, 0)
    for t in range(CHUNKS - 1):
        y_copy(t).wait_recv()

    def add(i, _):
        rows = pl.ds(pl.multiple_of(i * 16, 16), 16)
        acc = rsend[CHUNKS - 1, rows, :].astype(f32)
        for t in range(CHUNKS - 1):
            acc = acc + rrecv[t, rows, :].astype(f32)
        total[rows, :] = acc
        return 0

    lax.fori_loop(0, N // 16, add, 0)

    target = core * 4 + y
    slot = x * RING + spot
    packed[FILLED:PACKED, :] = jnp.zeros((PACKED - FILLED, 128), f32)

    def f_copy(to):
        return pltpu.make_async_remote_copy(
            src_ref=fsend.at[to], dst_ref=frecv.at[slot],
            send_sem=fs_sem.at[to], recv_sem=fr_sem.at[slot],
            device_id={"state": target, "slab": to}, device_id_type=MESH)

    def is_own(to):
        return jnp.logical_and(to == slab, target == state)

    def pack(i, _):
        q = lax.rem(slab // 4 + 4 + i, 8)
        for i in range(4):
            to = q * 4 + i
            for b in range(5):
                rows = total[pl.ds(pl.multiple_of(q * 40, 8), 40), 128 * b : 128 * (b + 1)]
                packed[b * 10 : b * 10 + 10, :] = rows[10 * i : 10 * i + 10]
            fsend[to] = packed[...].astype(bf16)

            @pl.when(is_own(to))
            def _():
                pltpu.make_async_copy(fsend.at[slab], frecv.at[slot], fr_sem.at[slot]).start()

            @pl.when(jnp.logical_not(is_own(to)))
            def _():
                f_copy(to).start()

        return 0

    lax.fori_loop(0, 8, pack, 0)

    def sent(t, _):
        for u in range(3):
            for copy in x_copies(t, u)[0] + z_copies(t, u)[0]:
                copy.wait_send()
        return 0

    lax.fori_loop(0, CHUNKS, sent, 0)
    for t in range(CHUNKS - 1):
        y_copy(t).wait_send()

    for coef in range(2):
        for h in range(2):
            for at in range(RING):
                i = (coef * 2 + h) * RING + at
                pltpu.make_async_copy(fsend.at[0], frecv.at[i], fr_sem.at[i]).wait()
                packed[...] = frecv[i].astype(f32)
                for b in range(5):
                    piece = packed[b * 10 : b * 10 + 10, :]
                    base = coef * N + 8 * h + at
                    if b < 4:
                        final[b // 2, pl.ds(base + 16 * (b % 2), 10, stride=32), :] = piece
                    else:
                        final[2, pl.ds(base, 10, stride=32), :] = piece
                        final[2, pl.ds(base + 16, 10, stride=32), :] = pltpu.roll(piece, 64, 1)
    out[:, 0:128] = final[0]
    out[:, 128:256] = final[1]
    out[:, 256:320] = final[2][:, :64]

    def left(to, _):
        @pl.when(jnp.logical_not(is_own(to)))
        def _():
            f_copy(to).wait_send()

        return 0

    lax.fori_loop(0, 32, left, 0)


def body(state_images, rot_index, counts):
    fwd, inv, fwd3, fz, gz, shifts = host_tables()
    image = state_images.reshape(2, 10, 2 * N, 128)
    smem = pl.BlockSpec(memory_space=pltpu.SMEM)
    anywhere = pl.BlockSpec(memory_space=pl.ANY)
    dma = pltpu.SemaphoreType.DMA
    vmem = pltpu.VMEM
    out = pl.pallas_call(
        kernel,
        name="shears",
        out_shape=jax.ShapeDtypeStruct((640, N), f32),
        in_specs=[anywhere, anywhere, smem] + [anywhere] * 6,
        out_specs=pl.BlockSpec(memory_space=vmem),
        scratch_shapes=[
            pltpu.SMEM((1,), jnp.int32), pltpu.SMEM((1,), jnp.int32),
            vmem(image.shape, bf16), vmem((2, 10, 128, LANES), bf16), vmem(fwd.shape, bf16), vmem(inv.shape, bf16),
            vmem(fwd3.shape, bf16), vmem(fz.shape, bf16), vmem(gz.shape, bf16),
            vmem((16, PAD), f32), vmem((16, PAD), f32),
            vmem((2 * N, PAD), f32), vmem((2 * N, PAD), f32), vmem((2 * N, PAD), f32), vmem((2 * N, PAD), f32),
            vmem((8, 4, BLOCK, LANES), bf16),
            vmem((CHUNKS, 8, BLOCK, LANES), bf16),
            vmem((CHUNKS, RING, BLOCK, LANES), bf16),
            vmem((CHUNKS, 2, N, LANES), bf16),
            vmem((CHUNKS, N, LANES), bf16),
            vmem((CHUNKS - 1, N, LANES), bf16),
            vmem((32, PACKED, 128), bf16),
            vmem((32, PACKED, 128), bf16),
            vmem((2, 8, 128), f32),
            vmem((5, 640, 128), f32),
            vmem((2 * N, LANES), bf16),
            vmem((N, LANES), f32),
            vmem((PACKED, 128), f32),
            vmem((3, 640, 128), f32),
            dma((5,)), dma((7,)), dma((CHUNKS, 3)), dma((CHUNKS, 3)), dma, dma,
            dma((CHUNKS, 3, 7)), dma((CHUNKS, 3, 7)),
            dma((CHUNKS, 3, RING - 1)), dma((CHUNKS, 3, RING - 1)),
            dma((CHUNKS - 1,)), dma((CHUNKS - 1,)),
            dma((32,)), dma((32,)),
        ],
        compiler_params=pltpu.CompilerParams(
            collective_id=0, has_side_effects=True, vmem_limit_bytes=60 * 1024 * 1024),
        cost_estimate=pl.CostEstimate(flops=13_000_000_000, bytes_accessed=8_000_000, transcendentals=0),
    )(rot_index, counts, shifts, image, fwd, inv, fwd3, fz, gz)
    return out.reshape(2, 10, 2, 16, N).swapaxes(3, 4)


def solution(mesh):
    placed = (P("state", None, "slab", None, None, None), P("state"), P("state"))
    return jax.shard_map(
        body,
        mesh=mesh,
        in_specs=placed,
        out_specs=P(None, "slab", None, None, "state"),
        check_vma=False,
    )
```

```python
import math

import jax
import jax.numpy as jnp
import numpy as np
from jax import lax
from jax.experimental import pallas as pl
from jax.experimental.pallas import tpu as pltpu
from jax.sharding import PartitionSpec as P

N = 320
HALF = N // 2
ANGLES = 32
LANES = 640
PAD = 384
WIDE = 2 * PAD
BLOCK = 80
CHUNKS = 4
UNITS = (2, 0, 1)
PACKED = 64
FILLED = 50
RING = 8
MESH = pl.DeviceIdType.MESH
f32 = jnp.float32
bf16 = jnp.bfloat16


def packed_lane(part, x):
    return np.where(x < 256, x // 128 * 256 + part * 128 + x % 128, 512 + part * 64 + (x - 256))


def host_tables():
    points = np.arange(N)
    phase = (points[:, None] * points[None, :] % N) * (2.0 * math.pi / N)
    cosine = np.cos(phase)
    sine = np.sin(phase)
    forward = np.zeros((2, N, 2, PAD))
    forward[0, :, 0, :N] = cosine
    forward[1, :, 0, :N] = sine
    forward[0, :, 1, :N] = -sine
    forward[1, :, 1, :N] = cosine
    forward = forward.reshape(2 * N, WIDE)
    inverse = np.zeros((2, PAD, 2, N))
    inverse[0, :N, 0] = cosine / N
    inverse[1, :N, 0] = -sine / N
    inverse[0, :N, 1] = sine / N
    inverse[1, :N, 1] = cosine / N
    inverse = inverse.reshape(WIDE, 2 * N)
    order = np.zeros(2 * N, np.int64)
    for part in range(2):
        order[packed_lane(part, points)] = part * N + points
    angle = -(np.arange(ANGLES) - ANGLES // 2) * math.pi / 120.0
    shifts = np.stack([-np.tan(angle / 2.0), np.sin(angle)])
    return (
        jnp.asarray(forward.astype(jnp.bfloat16)),
        jnp.asarray(inverse[:, order].astype(jnp.bfloat16)),
        jnp.asarray(forward[order].astype(jnp.bfloat16)),
        jnp.asarray(np.concatenate([cosine, sine]).astype(jnp.bfloat16)),
        jnp.asarray((np.concatenate([cosine, sine]) / N).astype(jnp.bfloat16)),
        jnp.asarray(shifts.astype(np.float32)),
    )


def turn(turns):
    half = (turns - jnp.floor(turns + 0.5)) * math.pi
    sq = half * half
    s = -1.0 / 39916800.0
    for c in (1.0 / 362880.0, -1.0 / 5040.0, 1.0 / 120.0, -1.0 / 6.0, 1.0):
        s = s * sq + c
    s = s * half
    c = 1.0 / 479001600.0
    for k in (-1.0 / 3628800.0, 1.0 / 40320.0, -1.0 / 720.0, 1.0 / 24.0, -0.5, 1.0):
        c = c * sq + k
    return 1.0 - 2.0 * s * s, 2.0 * s * c


def centred(index):
    return jnp.where(index >= HALF, index - N, index).astype(f32)


def unit_lanes(u):
    return slice(256 * u, 256 * u + (256 if u < 2 else 128))


def kernel(
    rot_hbm, counts_hbm, shifts, image, fwd_hbm, inv_hbm, fwd3_hbm, fz_hbm, gz_hbm,
    out,
    rot, counts, v, vt, fwd, inv, fwd3, fz, gz,
    cos_f, sin_f, cos_x, sin_x, cos_z, sin_z,
    xsend, xrecv, zsend, planes, rsend, rrecv, fsend, frecv,
    params, turned, second, total, packed, final,
    image_sem, load_sem, xl_sem, zl_sem, ps_sem, pr_sem,
    xs_sem, xr_sem, zs_sem, zr_sem, ys_sem, yr_sem, fs_sem, fr_sem,
):
    state = lax.axis_index("state")
    slab = lax.axis_index("slab")
    zlo = state // 4
    y = state % 4
    zhi = slab // 8
    x = (slab % 8) // 2
    core = slab % 2
    me = slab % 8
    spot = zhi * 2 + zlo

    def image_load(i):
        part = pl.ds(2 * i, 2)
        return pltpu.make_async_copy(image.at[:, part], v.at[:, part], image_sem.at[i])

    loads = [
        pltpu.make_async_copy(src, dst, load_sem.at[i])
        for i, (src, dst) in enumerate(
            ((rot_hbm, rot), (counts_hbm, counts), (fwd_hbm, fwd), (inv_hbm, inv),
             (fz_hbm, fz), (gz_hbm, gz), (fwd3_hbm, fwd3))
        )
    ]
    for copy in loads[:2]:
        copy.start()
    for i in range(5):
        image_load(i).start()

    barrier = pltpu.get_barrier_semaphore()

    def greet(i, _):
        to = lax.rem(slab + i, 32)
        for other in range(2):
            pl.semaphore_signal(
                barrier, inc=1,
                device_id={"state": other * 4 + y, "slab": to},
                device_id_type=MESH,
            )
        return 0

    lax.fori_loop(1, 32, greet, 0)
    pl.semaphore_signal(barrier, inc=1, device_id={"state": (1 - zlo) * 4 + y}, device_id_type=MESH)
    for i in range(1, 4):
        pl.semaphore_signal(
            barrier, inc=1, device_id={"state": zlo * 4 + lax.rem(y + i, 4)}, device_id_type=MESH)
    for copy in loads[2:]:
        copy.start()

    for copy in loads[:2]:
        copy.wait()
    tilt = shifts[0, rot[0]]
    lift = shifts[1, rot[0]]
    weight = counts[0].astype(f32) * (1.0 / 64.0)
    centre = (N - 1) / 2.0

    row = lax.broadcasted_iota(jnp.int32, (16, PAD), 0) + slab * 10
    freq = centred(lax.broadcasted_iota(jnp.int32, (16, PAD), 1)) * (1.0 / N)
    cosine, sine = turn(freq * (tilt * (row.astype(f32) - centre)))
    cos_f[...] = cosine
    sin_f[...] = sine

    row8 = lax.broadcasted_iota(jnp.int32, (8, 128), 0)
    params[zlo] = jnp.where(row8 == 0, tilt, jnp.where(row8 == 1, lift, weight))
    swap_params = pltpu.make_async_remote_copy(
        src_ref=params.at[zlo], dst_ref=params.at[zlo], send_sem=ps_sem, recv_sem=pr_sem,
        device_id={"state": (1 - zlo) * 4 + y}, device_id_type=MESH)

    def turn_image(i, _):
        image_load(i).wait()
        for coef in range(2):
            for j in range(2):
                vt[coef, 2 * i + j] = v[coef, 2 * i + j].T
        return 0

    lax.fori_loop(0, 5, turn_image, 0)
    for copy in loads[2:4]:
        copy.wait()

    def chunk_y(t):
        return lax.rem(y + 1 + t, 4)

    def first(t):
        yy = chunk_y(t)
        left = jnp.concatenate(
            [vt[coef, z, pl.ds(pl.multiple_of(64 * low + 16 * yy, 16), 16), :]
             for z in range(10) for coef in range(2) for low in range(2)], axis=0)
        spectrum = jnp.dot(left, fwd[...], preferred_element_type=f32)
        ramped = []
        for z in range(10):
            cosine = jnp.broadcast_to(cos_f[z : z + 1, :], (64, PAD))
            sine = jnp.broadcast_to(sin_f[z : z + 1, :], (64, PAD))
            re = spectrum[64 * z : 64 * (z + 1), :PAD]
            im = spectrum[64 * z : 64 * (z + 1), PAD:]
            ramped.append(
                jnp.concatenate([re * cosine + im * sine, im * cosine - re * sine], axis=1).astype(bf16))
        moved = jnp.dot(jnp.concatenate(ramped, axis=0), inv[...], preferred_element_type=f32)
        for pair in range(5):
            for coef in range(2):
                for low in range(2):
                    for h in range(2):
                        q = 128 * pair + 32 * coef + 16 * low + 8 * h
                        piece = jnp.concatenate([moved[q : q + 8], moved[q + 64 : q + 72]], axis=0)
                        xsend[(coef * 2 + h) * 2 + low, t, 16 * pair : 16 * (pair + 1), :] = piece.astype(bf16)

    def x_copies(t, u):
        lanes = unit_lanes(u)
        lanes = pl.ds(lanes.start, lanes.stop - lanes.start)
        out_copies = []
        for o in range(1, 8):
            gx = lax.rem(x + o // 2, 4)
            gc = lax.rem(core + o, 2)
            out_copies.append(pltpu.make_async_remote_copy(
                src_ref=xsend.at[gx * 2 + gc, t, :, lanes], dst_ref=xrecv.at[t, me, :, lanes],
                send_sem=xs_sem.at[t, u, o - 1], recv_sem=xr_sem.at[t, u, o - 1],
                device_id={"slab": zhi * 8 + gx * 2 + gc}, device_id_type=MESH))
        return out_copies, lambda: pltpu.make_async_copy(
            xsend.at[me, t, :, lanes], xrecv.at[t, me, :, lanes], xl_sem.at[t, u])

    def z_copies(t, u):
        lanes = unit_lanes(u)
        lanes = pl.ds(lanes.start, lanes.stop - lanes.start)
        out_copies = []
        dst = planes.at[t, zlo, pl.ds(pl.multiple_of(zhi * BLOCK, 16), BLOCK), lanes]
        for o in (4, 3, 5, 2, 6, 1, 7):
            to = lax.rem(spot + o, RING)
            out_copies.append(pltpu.make_async_remote_copy(
                src_ref=zsend.at[t, to, :, lanes], dst_ref=dst,
                send_sem=zs_sem.at[t, u, o - 1], recv_sem=zr_sem.at[t, u, o - 1],
                device_id={"state": (to % 2) * 4 + y, "slab": (to // 2) * 8 + me}, device_id_type=MESH))
        return out_copies, lambda: pltpu.make_async_copy(zsend.at[t, spot, :, lanes], dst, zl_sem.at[t, u])

    def y_copy(t):
        return pltpu.make_async_remote_copy(
            src_ref=rsend.at[t], dst_ref=rrecv.at[t],
            send_sem=ys_sem.at[t], recv_sem=yr_sem.at[t],
            device_id={"state": zlo * 4 + chunk_y(t)}, device_id_type=MESH)

    def start(copies):
        remote, own = copies
        for copy in remote:
            copy.start()
        own().start()

    def arrive(copies):
        remote, own = copies
        own().wait()
        for copy in remote:
            copy.wait_recv()

    first(0)
    pl.semaphore_wait(barrier, 66)
    start(x_copies(0, UNITS[0]))
    swap_params.start()
    start(x_copies(0, UNITS[1]))
    for copy in loads[4:]:
        copy.wait()
    swap_params.wait()

    def tables(i, _):
        row = lax.broadcasted_iota(jnp.int32, (16, 128), 0) + i * 16
        for s in range(2):
            rows = pl.ds(pl.multiple_of(s * N + i * 16, 16), 16)
            tilt_s = params[s, 0:1, :]
            lift_s = params[s, 1:2, :]
            for tile in range(3):
                lanes = slice(128 * tile, 128 * (tile + 1))
                lane = lax.broadcasted_iota(jnp.int32, (16, 128), 1) + 128 * tile
                cosine, sine = turn(centred(lane) * (tilt_s * (row.astype(f32) - centre)) * (1.0 / N))
                cos_x[rows, lanes] = cosine
                sin_x[rows, lanes] = sine
                at = jnp.where(lane >= N, lane - 64, lane)
                cosine, sine = turn(centred(row) * (lift_s * (at.astype(f32) - centre)) * (1.0 / N))
                cos_z[rows, lanes] = cosine
                sin_z[rows, lanes] = sine
        return 0

    def transpose(t, u):
        lanes = unit_lanes(u)
        for lane in range(lanes.start // 128, lanes.stop // 128):
            for g in range(8):
                turned[lane, BLOCK * g : BLOCK * (g + 1), :] = xrecv[
                    t, g, :, 128 * lane : 128 * (lane + 1)].astype(f32)
        for lane in range(lanes.start // 128, lanes.stop // 128):
            for m in range(8):
                zsend[t, m, :, 128 * lane : 128 * (lane + 1)] = turned[
                    lane, pl.ds(m, BLOCK, stride=8), :].astype(bf16)

    lane128 = lax.broadcasted_iota(jnp.int32, (N, 128), 1)

    def swap(left, right, paired):
        if paired:
            return right, -left
        l = pltpu.roll(left, 64, 1)
        r = pltpu.roll(right, 64, 1)
        return jnp.where(lane128 < 64, l, -l), jnp.where(lane128 < 64, r, -r)

    def shear_z(t, u):
        if u < 2:
            pairs = [((s, 2 * u), (s, 2 * u + 1)) for s in range(2)]
        else:
            pairs = [((0, 4), (1, 4))]
        for pair in pairs:
            data = jnp.concatenate([planes[t, s, :, 128 * b : 128 * (b + 1)] for s, b in pair], axis=1)
            both = jnp.dot(fz[...], data, preferred_element_type=f32)
            near, far = [], []
            for i, (s, b) in enumerate(pair):
                cosine = cos_z[s * N : (s + 1) * N, 128 * u : 128 * (u + 1)]
                sine = sin_z[s * N : (s + 1) * N, 128 * u : 128 * (u + 1)]
                tc = both[:N, 128 * i : 128 * (i + 1)]
                ts = both[N:, 128 * i : 128 * (i + 1)]
                near.append(cosine * tc - sine * ts)
                far.append(cosine * ts + sine * tc)
            far = swap(far[0], far[1], u < 2)
            ramped = jnp.concatenate([near[0] + far[0], near[1] + far[1]], axis=1).astype(bf16)
            both = jnp.dot(gz[...], ramped, preferred_element_type=f32)
            far = swap(both[N:, :128], both[N:, 128:], u < 2)
            for i, (s, b) in enumerate(pair):
                second[s * N : (s + 1) * N, 128 * b : 128 * (b + 1)] = (
                    both[:N, 128 * i : 128 * (i + 1)] - far[i]).astype(bf16)

    def shear_x(t):
        spectrum = jnp.dot(second[...], fwd3[...], preferred_element_type=f32)
        re, im = spectrum[:, :PAD], spectrum[:, PAD:]
        cosine, sine = cos_x[...], sin_x[...]
        ramped = jnp.concatenate([re * cosine + im * sine, im * cosine - re * sine], axis=1).astype(bf16)
        moved = jnp.dot(ramped, inv[...], preferred_element_type=f32)
        w0 = jnp.concatenate([params[0, 2:3, :]] * 5, axis=1)
        w1 = jnp.concatenate([params[1, 2:3, :]] * 5, axis=1)
        rsend[t] = (moved[:N] * w0 + moved[N:] * w1).astype(bf16)

    def step(t, _):
        @pl.when(t < CHUNKS)
        def _():
            for i, u in enumerate(UNITS):
                arrive(x_copies(t, u))
                transpose(t, u)
                start(z_copies(t, u))
                if i == 0:
                    @pl.when(t == 0)
                    def _():
                        start(x_copies(0, UNITS[2]))

                    @pl.when(t < CHUNKS - 1)
                    def _():
                        first(t + 1)

                @pl.when(t < CHUNKS - 1)
                def _():
                    start(x_copies(t + 1, u))

        @pl.when(t == 0)
        def _():
            lax.fori_loop(0, N // 16, tables, 0)

        @pl.when(t >= 1)
        def _():
            for u in UNITS:
                arrive(z_copies(t - 1, u))
                shear_z(t - 1, u)
            shear_x(t - 1)

            @pl.when(t < CHUNKS)
            def _():
                y_copy(t - 1).start()

        return 0

    lax.fori_loop(0, CHUNKS + 1, step, 0)
    for t in range(CHUNKS - 1):
        y_copy(t).wait_recv()

    def add(i, _):
        rows = pl.ds(pl.multiple_of(i * 16, 16), 16)
        acc = rsend[CHUNKS - 1, rows, :].astype(f32)
        for t in range(CHUNKS - 1):
            acc = acc + rrecv[t, rows, :].astype(f32)
        total[rows, :] = acc
        return 0

    lax.fori_loop(0, N // 16, add, 0)

    target = core * 4 + y
    slot = x * RING + spot
    packed[FILLED:PACKED, :] = jnp.zeros((PACKED - FILLED, 128), f32)

    def f_copy(to):
        return pltpu.make_async_remote_copy(
            src_ref=fsend.at[to], dst_ref=frecv.at[slot],
            send_sem=fs_sem.at[to], recv_sem=fr_sem.at[slot],
            device_id={"state": target, "slab": to}, device_id_type=MESH)

    def is_own(to):
        return jnp.logical_and(to == slab, target == state)

    def pack(i, _):
        q = lax.rem(slab // 4 + 4 + i, 8)
        for i in range(4):
            to = q * 4 + i
            for b in range(5):
                rows = total[pl.ds(pl.multiple_of(q * 40, 8), 40), 128 * b : 128 * (b + 1)]
                packed[b * 10 : b * 10 + 10, :] = rows[10 * i : 10 * i + 10]
            fsend[to] = packed[...].astype(bf16)

            @pl.when(is_own(to))
            def _():
                pltpu.make_async_copy(fsend.at[slab], frecv.at[slot], fr_sem.at[slot]).start()

            @pl.when(jnp.logical_not(is_own(to)))
            def _():
                f_copy(to).start()

        return 0

    lax.fori_loop(0, 8, pack, 0)

    def sent(t, _):
        for u in range(3):
            for copy in x_copies(t, u)[0] + z_copies(t, u)[0]:
                copy.wait_send()
        return 0

    lax.fori_loop(0, CHUNKS, sent, 0)
    for t in range(CHUNKS - 1):
        y_copy(t).wait_send()

    for coef in range(2):
        for h in range(2):
            for at in range(RING):
                i = (coef * 2 + h) * RING + at
                pltpu.make_async_copy(fsend.at[0], frecv.at[i], fr_sem.at[i]).wait()
                packed[...] = frecv[i].astype(f32)
                for b in range(5):
                    piece = packed[b * 10 : b * 10 + 10, :]
                    base = coef * N + 8 * h + at
                    if b < 4:
                        final[b // 2, pl.ds(base + 16 * (b % 2), 10, stride=32), :] = piece
                    else:
                        final[2, pl.ds(base, 10, stride=32), :] = piece
                        final[2, pl.ds(base + 16, 10, stride=32), :] = pltpu.roll(piece, 64, 1)
    out[:, 0:128] = final[0]
    out[:, 128:256] = final[1]
    out[:, 256:320] = final[2][:, :64]

    def left(to, _):
        @pl.when(jnp.logical_not(is_own(to)))
        def _():
            f_copy(to).wait_send()

        return 0

    lax.fori_loop(0, 32, left, 0)


def body(state_images, rot_index, counts):
    fwd, inv, fwd3, fz, gz, shifts = host_tables()
    image = state_images.reshape(2, 10, 2 * N, 128)
    smem = pl.BlockSpec(memory_space=pltpu.SMEM)
    anywhere = pl.BlockSpec(memory_space=pl.ANY)
    dma = pltpu.SemaphoreType.DMA
    vmem = pltpu.VMEM
    out = pl.pallas_call(
        kernel,
        name="shears",
        out_shape=jax.ShapeDtypeStruct((640, N), f32),
        in_specs=[anywhere, anywhere, smem] + [anywhere] * 6,
        out_specs=pl.BlockSpec(memory_space=vmem),
        scratch_shapes=[
            pltpu.SMEM((1,), jnp.int32), pltpu.SMEM((1,), jnp.int32),
            vmem(image.shape, bf16), vmem((2, 10, 128, LANES), bf16), vmem(fwd.shape, bf16), vmem(inv.shape, bf16),
            vmem(fwd3.shape, bf16), vmem(fz.shape, bf16), vmem(gz.shape, bf16),
            vmem((16, PAD), f32), vmem((16, PAD), f32),
            vmem((2 * N, PAD), f32), vmem((2 * N, PAD), f32), vmem((2 * N, PAD), f32), vmem((2 * N, PAD), f32),
            vmem((8, 4, BLOCK, LANES), bf16),
            vmem((CHUNKS, 8, BLOCK, LANES), bf16),
            vmem((CHUNKS, RING, BLOCK, LANES), bf16),
            vmem((CHUNKS, 2, N, LANES), bf16),
            vmem((CHUNKS, N, LANES), bf16),
            vmem((CHUNKS - 1, N, LANES), bf16),
            vmem((32, PACKED, 128), bf16),
            vmem((32, PACKED, 128), bf16),
            vmem((2, 8, 128), f32),
            vmem((5, 640, 128), f32),
            vmem((2 * N, LANES), bf16),
            vmem((N, LANES), f32),
            vmem((PACKED, 128), f32),
            vmem((3, 640, 128), f32),
            dma((5,)), dma((7,)), dma((CHUNKS, 3)), dma((CHUNKS, 3)), dma, dma,
            dma((CHUNKS, 3, 7)), dma((CHUNKS, 3, 7)),
            dma((CHUNKS, 3, RING - 1)), dma((CHUNKS, 3, RING - 1)),
            dma((CHUNKS - 1,)), dma((CHUNKS - 1,)),
            dma((32,)), dma((32,)),
        ],
        compiler_params=pltpu.CompilerParams(
            collective_id=0, has_side_effects=True, vmem_limit_bytes=60 * 1024 * 1024),
        cost_estimate=pl.CostEstimate(flops=13_000_000_000, bytes_accessed=8_000_000, transcendentals=0),
    )(rot_index, counts, shifts, image, fwd, inv, fwd3, fz, gz)
    return out.reshape(2, 10, 2, 16, N).swapaxes(3, 4)


def solution(mesh):
    placed = (P("state", None, "slab", None, None, None), P("state"), P("state"))
    return jax.shard_map(
        body,
        mesh=mesh,
        in_specs=placed,
        out_specs=P(None, "slab", None, None, "state"),
        check_vma=False,
    )
```

```python
import math

import jax
import jax.numpy as jnp
import numpy as np
from jax import lax
from jax.experimental import pallas as pl
from jax.experimental.pallas import tpu as pltpu
from jax.sharding import PartitionSpec as P

N = 320
HALF = N // 2
ANGLES = 32
LANES = 640
PAD = 384
WIDE = 2 * PAD
BLOCK = 80
CHUNKS = 4
UNITS = (2, 0, 1)
PACKED = 64
FILLED = 50
RING = 8
MESH = pl.DeviceIdType.MESH
f32 = jnp.float32
bf16 = jnp.bfloat16


def packed_lane(part, x):
    return np.where(x < 256, x // 128 * 256 + part * 128 + x % 128, 512 + part * 64 + (x - 256))


def host_tables():
    points = np.arange(N)
    phase = (points[:, None] * points[None, :] % N) * (2.0 * math.pi / N)
    cosine = np.cos(phase)
    sine = np.sin(phase)
    forward = np.zeros((2, N, 2, PAD))
    forward[0, :, 0, :N] = cosine
    forward[1, :, 0, :N] = sine
    forward[0, :, 1, :N] = -sine
    forward[1, :, 1, :N] = cosine
    forward = forward.reshape(2 * N, WIDE)
    inverse = np.zeros((2, PAD, 2, N))
    inverse[0, :N, 0] = cosine / N
    inverse[1, :N, 0] = -sine / N
    inverse[0, :N, 1] = sine / N
    inverse[1, :N, 1] = cosine / N
    inverse = inverse.reshape(WIDE, 2 * N)
    order = np.zeros(2 * N, np.int64)
    for part in range(2):
        order[packed_lane(part, points)] = part * N + points
    angle = -(np.arange(ANGLES) - ANGLES // 2) * math.pi / 120.0
    shifts = np.stack([-np.tan(angle / 2.0), np.sin(angle)])
    return (
        jnp.asarray(forward.astype(jnp.bfloat16)),
        jnp.asarray(inverse[:, order].astype(jnp.bfloat16)),
        jnp.asarray(forward[order].astype(jnp.bfloat16)),
        jnp.asarray(np.concatenate([cosine, sine]).astype(jnp.bfloat16)),
        jnp.asarray((np.concatenate([cosine, sine]) / N).astype(jnp.bfloat16)),
        jnp.asarray(shifts.astype(np.float32)),
    )


def turn(turns):
    half = (turns - jnp.floor(turns + 0.5)) * math.pi
    sq = half * half
    s = -1.0 / 39916800.0
    for c in (1.0 / 362880.0, -1.0 / 5040.0, 1.0 / 120.0, -1.0 / 6.0, 1.0):
        s = s * sq + c
    s = s * half
    c = 1.0 / 479001600.0
    for k in (-1.0 / 3628800.0, 1.0 / 40320.0, -1.0 / 720.0, 1.0 / 24.0, -0.5, 1.0):
        c = c * sq + k
    return 1.0 - 2.0 * s * s, 2.0 * s * c


def centred(index):
    return jnp.where(index >= HALF, index - N, index).astype(f32)


def unit_lanes(u):
    return slice(256 * u, 256 * u + (256 if u < 2 else 128))


def kernel(
    rot_hbm, counts_hbm, shifts, image, fwd_hbm, inv_hbm, fwd3_hbm, fz_hbm, gz_hbm,
    out,
    rot, counts, v, vt, fwd, inv, fwd3, fz, gz,
    cos_f, sin_f, cos_x, sin_x, cos_z, sin_z,
    xsend, xrecv, zsend, planes, rsend, rrecv, fsend, frecv,
    params, turned, second, total, packed, final,
    ready, image_sem, load_sem, xl_sem, zl_sem, ps_sem, pr_sem,
    xs_sem, xr_sem, zs_sem, zr_sem, ys_sem, yr_sem, fs_sem, fr_sem,
):
    state = lax.axis_index("state")
    slab = lax.axis_index("slab")
    zlo = state // 4
    y = state % 4
    zhi = slab // 8
    x = (slab % 8) // 2
    core = slab % 2
    me = slab % 8
    spot = zhi * 2 + zlo

    def image_load(i):
        part = pl.ds(2 * i, 2)
        return pltpu.make_async_copy(image.at[:, part], v.at[:, part], image_sem.at[i])

    loads = [
        pltpu.make_async_copy(src, dst, load_sem.at[i])
        for i, (src, dst) in enumerate(
            ((rot_hbm, rot), (counts_hbm, counts), (fwd_hbm, fwd), (inv_hbm, inv),
             (fz_hbm, fz), (gz_hbm, gz), (fwd3_hbm, fwd3))
        )
    ]
    for copy in loads[:2]:
        copy.start()
    for i in range(5):
        image_load(i).start()

    barrier = pltpu.get_barrier_semaphore()

    def ring(o):
        to = lax.rem(spot + o, RING)
        return {"state": (to % 2) * 4 + y, "slab": (to // 2) * 8 + me}

    for o in range(1, 8):
        pl.semaphore_signal(
            barrier, inc=1, device_id={"slab": zhi * 8 + lax.rem(me + o, 8)}, device_id_type=MESH)
    for o in range(1, RING):
        pl.semaphore_signal(barrier, inc=1, device_id=ring(o), device_id_type=MESH)
    for o in range(1, 4):
        pl.semaphore_signal(
            barrier, inc=1, device_id={"state": zlo * 4 + lax.rem(y + o, 4)}, device_id_type=MESH)
    for copy in loads[2:4]:
        copy.start()

    for copy in loads[:2]:
        copy.wait()
    tilt = shifts[0, rot[0]]
    lift = shifts[1, rot[0]]
    weight = counts[0].astype(f32) * (1.0 / 64.0)
    centre = (N - 1) / 2.0

    row = lax.broadcasted_iota(jnp.int32, (16, PAD), 0) + slab * 10
    freq = centred(lax.broadcasted_iota(jnp.int32, (16, PAD), 1)) * (1.0 / N)
    cosine, sine = turn(freq * (tilt * (row.astype(f32) - centre)))
    cos_f[...] = cosine
    sin_f[...] = sine

    row8 = lax.broadcasted_iota(jnp.int32, (8, 128), 0)
    params[zlo] = jnp.where(row8 == 0, tilt, jnp.where(row8 == 1, lift, weight))
    swap_params = pltpu.make_async_remote_copy(
        src_ref=params.at[zlo], dst_ref=params.at[zlo], send_sem=ps_sem, recv_sem=pr_sem,
        device_id={"state": (1 - zlo) * 4 + y}, device_id_type=MESH)

    def turn_image(i, _):
        image_load(i).wait()
        for coef in range(2):
            for j in range(2):
                vt[coef, 2 * i + j] = v[coef, 2 * i + j].T
        return 0

    lax.fori_loop(0, 5, turn_image, 0)
    for copy in loads[2:4]:
        copy.wait()

    def chunk_y(t):
        return lax.rem(y + 1 + t, 4)

    def first(t):
        yy = chunk_y(t)
        left = jnp.concatenate(
            [vt[coef, z, pl.ds(pl.multiple_of(64 * low + 16 * yy, 16), 16), :]
             for z in range(10) for coef in range(2) for low in range(2)], axis=0)
        spectrum = jnp.dot(left, fwd[...], preferred_element_type=f32)
        ramped = []
        for z in range(10):
            cosine = jnp.broadcast_to(cos_f[z : z + 1, :], (64, PAD))
            sine = jnp.broadcast_to(sin_f[z : z + 1, :], (64, PAD))
            re = spectrum[64 * z : 64 * (z + 1), :PAD]
            im = spectrum[64 * z : 64 * (z + 1), PAD:]
            ramped.append(
                jnp.concatenate([re * cosine + im * sine, im * cosine - re * sine], axis=1).astype(bf16))
        moved = jnp.dot(jnp.concatenate(ramped, axis=0), inv[...], preferred_element_type=f32)
        for pair in range(5):
            for coef in range(2):
                for low in range(2):
                    for h in range(2):
                        q = 128 * pair + 32 * coef + 16 * low + 8 * h
                        piece = jnp.concatenate([moved[q : q + 8], moved[q + 64 : q + 72]], axis=0)
                        xsend[(coef * 2 + h) * 2 + low, t, 16 * pair : 16 * (pair + 1), :] = piece.astype(bf16)

    def x_copies(t, u):
        lanes = unit_lanes(u)
        lanes = pl.ds(lanes.start, lanes.stop - lanes.start)
        out_copies = []
        for o in range(1, 8):
            gx = lax.rem(x + o // 2, 4)
            gc = lax.rem(core + o, 2)
            out_copies.append(pltpu.make_async_remote_copy(
                src_ref=xsend.at[gx * 2 + gc, t, :, lanes], dst_ref=xrecv.at[t, me, :, lanes],
                send_sem=xs_sem.at[t, u, o - 1], recv_sem=xr_sem.at[t, u, o - 1],
                device_id={"slab": zhi * 8 + gx * 2 + gc}, device_id_type=MESH))
        return out_copies, lambda: pltpu.make_async_copy(
            xsend.at[me, t, :, lanes], xrecv.at[t, me, :, lanes], xl_sem.at[t, u])

    def z_copies(t, u):
        lanes = unit_lanes(u)
        lanes = pl.ds(lanes.start, lanes.stop - lanes.start)
        out_copies = []
        dst = planes.at[t, zlo, pl.ds(pl.multiple_of(zhi * BLOCK, 16), BLOCK), lanes]
        for o in (4, 3, 5, 2, 6, 1, 7):
            to = lax.rem(spot + o, RING)
            out_copies.append(pltpu.make_async_remote_copy(
                src_ref=zsend.at[t, to, :, lanes], dst_ref=dst,
                send_sem=zs_sem.at[t, u, o - 1], recv_sem=zr_sem.at[t, u, o - 1],
                device_id={"state": (to % 2) * 4 + y, "slab": (to // 2) * 8 + me}, device_id_type=MESH))
        return out_copies, lambda: pltpu.make_async_copy(zsend.at[t, spot, :, lanes], dst, zl_sem.at[t, u])

    def y_copy(t):
        return pltpu.make_async_remote_copy(
            src_ref=rsend.at[t], dst_ref=rrecv.at[t],
            send_sem=ys_sem.at[t], recv_sem=yr_sem.at[t],
            device_id={"state": zlo * 4 + chunk_y(t)}, device_id_type=MESH)

    def start(copies):
        remote, own = copies
        for copy in remote:
            copy.start()
        own().start()

    def arrive(copies):
        remote, own = copies
        own().wait()
        for copy in remote:
            copy.wait_recv()

    first(0)
    pl.semaphore_wait(barrier, 2 * 7 + 3)
    start(x_copies(0, UNITS[0]))
    swap_params.start()
    start(x_copies(0, UNITS[1]))
    for o in range(1, RING):
        pl.semaphore_signal(ready, inc=1, device_id=ring(o), device_id_type=MESH)
    for copy in loads[4:]:
        copy.start()

    def tables(i, _):
        row = lax.broadcasted_iota(jnp.int32, (16, 128), 0) + i * 16
        for s in range(2):
            rows = pl.ds(pl.multiple_of(s * N + i * 16, 16), 16)
            tilt_s = params[s, 0:1, :]
            lift_s = params[s, 1:2, :]
            for tile in range(3):
                lanes = slice(128 * tile, 128 * (tile + 1))
                lane = lax.broadcasted_iota(jnp.int32, (16, 128), 1) + 128 * tile
                cosine, sine = turn(centred(lane) * (tilt_s * (row.astype(f32) - centre)) * (1.0 / N))
                cos_x[rows, lanes] = cosine
                sin_x[rows, lanes] = sine
                at = jnp.where(lane >= N, lane - 64, lane)
                cosine, sine = turn(centred(row) * (lift_s * (at.astype(f32) - centre)) * (1.0 / N))
                cos_z[rows, lanes] = cosine
                sin_z[rows, lanes] = sine
        return 0

    def transpose(t, u):
        lanes = unit_lanes(u)
        for lane in range(lanes.start // 128, lanes.stop // 128):
            for g in range(8):
                turned[lane, BLOCK * g : BLOCK * (g + 1), :] = xrecv[
                    t, g, :, 128 * lane : 128 * (lane + 1)].astype(f32)
        for lane in range(lanes.start // 128, lanes.stop // 128):
            for m in range(8):
                zsend[t, m, :, 128 * lane : 128 * (lane + 1)] = turned[
                    lane, pl.ds(m, BLOCK, stride=8), :].astype(bf16)

    lane128 = lax.broadcasted_iota(jnp.int32, (N, 128), 1)

    def swap(left, right, paired):
        if paired:
            return right, -left
        l = pltpu.roll(left, 64, 1)
        r = pltpu.roll(right, 64, 1)
        return jnp.where(lane128 < 64, l, -l), jnp.where(lane128 < 64, r, -r)

    def shear_z(t, u):
        if u < 2:
            pairs = [((s, 2 * u), (s, 2 * u + 1)) for s in range(2)]
        else:
            pairs = [((0, 4), (1, 4))]
        for pair in pairs:
            data = jnp.concatenate([planes[t, s, :, 128 * b : 128 * (b + 1)] for s, b in pair], axis=1)
            both = jnp.dot(fz[...], data, preferred_element_type=f32)
            near, far = [], []
            for i, (s, b) in enumerate(pair):
                cosine = cos_z[s * N : (s + 1) * N, 128 * u : 128 * (u + 1)]
                sine = sin_z[s * N : (s + 1) * N, 128 * u : 128 * (u + 1)]
                tc = both[:N, 128 * i : 128 * (i + 1)]
                ts = both[N:, 128 * i : 128 * (i + 1)]
                near.append(cosine * tc - sine * ts)
                far.append(cosine * ts + sine * tc)
            far = swap(far[0], far[1], u < 2)
            ramped = jnp.concatenate([near[0] + far[0], near[1] + far[1]], axis=1).astype(bf16)
            both = jnp.dot(gz[...], ramped, preferred_element_type=f32)
            far = swap(both[N:, :128], both[N:, 128:], u < 2)
            for i, (s, b) in enumerate(pair):
                second[s * N : (s + 1) * N, 128 * b : 128 * (b + 1)] = (
                    both[:N, 128 * i : 128 * (i + 1)] - far[i]).astype(bf16)

    def shear_x(t):
        spectrum = jnp.dot(second[...], fwd3[...], preferred_element_type=f32)
        re, im = spectrum[:, :PAD], spectrum[:, PAD:]
        cosine, sine = cos_x[...], sin_x[...]
        ramped = jnp.concatenate([re * cosine + im * sine, im * cosine - re * sine], axis=1).astype(bf16)
        moved = jnp.dot(ramped, inv[...], preferred_element_type=f32)
        w0 = jnp.concatenate([params[0, 2:3, :]] * 5, axis=1)
        w1 = jnp.concatenate([params[1, 2:3, :]] * 5, axis=1)
        rsend[t] = (moved[:N] * w0 + moved[N:] * w1).astype(bf16)

    def step(t, _):
        @pl.when(t < CHUNKS)
        def _():
            for i, u in enumerate(UNITS):
                arrive(x_copies(t, u))
                transpose(t, u)
                start(z_copies(t, u))
                if i == 0:
                    @pl.when(t == 0)
                    def _():
                        start(x_copies(0, UNITS[2]))

                    @pl.when(t < CHUNKS - 1)
                    def _():
                        first(t + 1)

                @pl.when(t < CHUNKS - 1)
                def _():
                    start(x_copies(t + 1, u))

        @pl.when(t == 0)
        def _():
            swap_params.wait()
            for copy in loads[4:]:
                copy.wait()
            lax.fori_loop(0, N // 16, tables, 0)

        @pl.when(t >= 1)
        def _():
            for u in UNITS:
                arrive(z_copies(t - 1, u))
                shear_z(t - 1, u)
            shear_x(t - 1)

            @pl.when(t < CHUNKS)
            def _():
                y_copy(t - 1).start()

        return 0

    lax.fori_loop(0, CHUNKS + 1, step, 0)
    for t in range(CHUNKS - 1):
        y_copy(t).wait_recv()

    target = core * 4 + y
    slot = x * RING + spot
    for g in range(8):
        packed[g, FILLED:PACKED, :] = jnp.zeros((PACKED - FILLED, 128), f32)

    def f_copy(to):
        return pltpu.make_async_remote_copy(
            src_ref=fsend.at[to], dst_ref=frecv.at[slot],
            send_sem=fs_sem.at[to], recv_sem=fr_sem.at[slot],
            device_id={"state": target, "slab": to}, device_id_type=MESH)

    def is_own(to):
        return jnp.logical_and(to == slab, target == state)

    def pack(i, _):
        block = lax.rem(zhi + 2 + i, 4)
        rows = pl.ds(pl.multiple_of(block * BLOCK, 16), BLOCK)
        for b in range(5):
            lanes = slice(128 * b, 128 * (b + 1))
            acc = rsend[CHUNKS - 1, rows, lanes].astype(f32)
            for t in range(CHUNKS - 1):
                acc = acc + rrecv[t, rows, lanes].astype(f32)
            total[b] = acc
        for g in range(8):
            to = block * 8 + g
            for b in range(5):
                packed[g, b * 10 : b * 10 + 10, :] = total[b, 10 * g : 10 * g + 10, :]
            fsend[to] = packed[g].astype(bf16)

            @pl.when(is_own(to))
            def _():
                pltpu.make_async_copy(fsend.at[slab], frecv.at[slot], fr_sem.at[slot]).start()

            @pl.when(jnp.logical_not(is_own(to)))
            def _():
                f_copy(to).start()

        return 0

    pl.semaphore_wait(ready, RING - 1)
    lax.fori_loop(0, 4, pack, 0)

    def sent(t, _):
        for u in range(3):
            for copy in x_copies(t, u)[0] + z_copies(t, u)[0]:
                copy.wait_send()
        return 0

    lax.fori_loop(0, CHUNKS, sent, 0)
    for t in range(CHUNKS - 1):
        y_copy(t).wait_send()

    for source in range(4):
        for at in range(RING):
            i = source * RING + at
            pltpu.make_async_copy(fsend.at[0], frecv.at[i], fr_sem.at[i]).wait()
            final[source, PACKED * at : PACKED * (at + 1), :] = frecv[i].astype(f32)
        for z in range(10):
            for b in range(5):
                rows = final[source, pl.ds(b * 10 + z, RING, stride=PACKED), :]
                base = (source // 2) * N + 32 * z + 8 * (source % 2)
                if b < 4:
                    base += 16 * (b % 2)
                    out[base : base + 8, 128 * (b // 2) : 128 * (b // 2 + 1)] = rows
                else:
                    out[base : base + 8, 256:320] = rows[:, :64]
                    out[base + 16 : base + 24, 256:320] = pltpu.roll(rows, 64, 1)[:, :64]

    def left(to, _):
        @pl.when(jnp.logical_not(is_own(to)))
        def _():
            f_copy(to).wait_send()

        return 0

    lax.fori_loop(0, 32, left, 0)


def body(state_images, rot_index, counts):
    fwd, inv, fwd3, fz, gz, shifts = host_tables()
    image = state_images.reshape(2, 10, 2 * N, 128)
    smem = pl.BlockSpec(memory_space=pltpu.SMEM)
    anywhere = pl.BlockSpec(memory_space=pl.ANY)
    dma = pltpu.SemaphoreType.DMA
    vmem = pltpu.VMEM
    out = pl.pallas_call(
        kernel,
        name="shears",
        out_shape=jax.ShapeDtypeStruct((640, N), f32),
        in_specs=[anywhere, anywhere, smem] + [anywhere] * 6,
        out_specs=pl.BlockSpec(memory_space=vmem),
        scratch_shapes=[
            pltpu.SMEM((1,), jnp.int32), pltpu.SMEM((1,), jnp.int32),
            vmem(image.shape, bf16), vmem((2, 10, 128, LANES), bf16), vmem(fwd.shape, bf16), vmem(inv.shape, bf16),
            vmem(fwd3.shape, bf16), vmem(fz.shape, bf16), vmem(gz.shape, bf16),
            vmem((16, PAD), f32), vmem((16, PAD), f32),
            vmem((2 * N, PAD), f32), vmem((2 * N, PAD), f32), vmem((2 * N, PAD), f32), vmem((2 * N, PAD), f32),
            vmem((8, 4, BLOCK, LANES), bf16),
            vmem((CHUNKS, 8, BLOCK, LANES), bf16),
            vmem((CHUNKS, RING, BLOCK, LANES), bf16),
            vmem((CHUNKS, 2, N, LANES), bf16),
            vmem((CHUNKS, N, LANES), bf16),
            vmem((CHUNKS - 1, N, LANES), bf16),
            vmem((32, PACKED, 128), bf16),
            vmem((32, PACKED, 128), bf16),
            vmem((2, 8, 128), f32),
            vmem((5, 640, 128), f32),
            vmem((2 * N, LANES), bf16),
            vmem((5, BLOCK, 128), f32),
            vmem((8, PACKED, 128), f32),
            vmem((4, RING * PACKED, 128), f32),
            pltpu.SemaphoreType.REGULAR, dma((5,)), dma((7,)), dma((CHUNKS, 3)), dma((CHUNKS, 3)), dma, dma,
            dma((CHUNKS, 3, 7)), dma((CHUNKS, 3, 7)),
            dma((CHUNKS, 3, RING - 1)), dma((CHUNKS, 3, RING - 1)),
            dma((CHUNKS - 1,)), dma((CHUNKS - 1,)),
            dma((32,)), dma((32,)),
        ],
        compiler_params=pltpu.CompilerParams(
            collective_id=0, has_side_effects=True, vmem_limit_bytes=60 * 1024 * 1024),
        cost_estimate=pl.CostEstimate(flops=13_000_000_000, bytes_accessed=8_000_000, transcendentals=0),
    )(rot_index, counts, shifts, image, fwd, inv, fwd3, fz, gz)
    return out.reshape(2, 10, 2, 16, N).swapaxes(3, 4)


def solution(mesh):
    placed = (P("state", None, "slab", None, None, None), P("state"), P("state"))
    return jax.shard_map(
        body,
        mesh=mesh,
        in_specs=placed,
        out_specs=P(None, "slab", None, None, "state"),
        check_vma=False,
    )
```

```python
import math

import jax
import jax.numpy as jnp
import numpy as np
from jax import lax
from jax.experimental import pallas as pl
from jax.experimental.pallas import tpu as pltpu
from jax.sharding import PartitionSpec as P

N = 320
HALF = N // 2
ANGLES = 32
LANES = 640
PAD = 384
WIDE = 2 * PAD
BLOCK = 80
CHUNKS = 4
UNITS = (2, 0, 1)
PACKED = 64
FILLED = 50
RING = 8
MESH = pl.DeviceIdType.MESH
f32 = jnp.float32
bf16 = jnp.bfloat16


def packed_lane(part, x):
    return np.where(x < 256, x // 128 * 256 + part * 128 + x % 128, 512 + part * 64 + (x - 256))


def host_tables():
    points = np.arange(N)
    phase = (points[:, None] * points[None, :] % N) * (2.0 * math.pi / N)
    cosine = np.cos(phase)
    sine = np.sin(phase)
    forward = np.zeros((2, N, 2, PAD))
    forward[0, :, 0, :N] = cosine
    forward[1, :, 0, :N] = sine
    forward[0, :, 1, :N] = -sine
    forward[1, :, 1, :N] = cosine
    forward = forward.reshape(2 * N, WIDE)
    inverse = np.zeros((2, PAD, 2, N))
    inverse[0, :N, 0] = cosine / N
    inverse[1, :N, 0] = -sine / N
    inverse[0, :N, 1] = sine / N
    inverse[1, :N, 1] = cosine / N
    inverse = inverse.reshape(WIDE, 2 * N)
    order = np.zeros(2 * N, np.int64)
    for part in range(2):
        order[packed_lane(part, points)] = part * N + points
    angle = -(np.arange(ANGLES) - ANGLES // 2) * math.pi / 120.0
    shifts = np.stack([-np.tan(angle / 2.0), np.sin(angle)])
    return (
        jnp.asarray(forward.astype(jnp.bfloat16)),
        jnp.asarray(inverse[:, order].astype(jnp.bfloat16)),
        jnp.asarray(forward[order].astype(jnp.bfloat16)),
        jnp.asarray(np.concatenate([cosine, sine]).astype(jnp.bfloat16)),
        jnp.asarray((np.concatenate([cosine, sine]) / N).astype(jnp.bfloat16)),
        jnp.asarray(shifts.astype(np.float32)),
    )


def turn(turns):
    half = (turns - jnp.floor(turns + 0.5)) * math.pi
    sq = half * half
    s = -1.0 / 39916800.0
    for c in (1.0 / 362880.0, -1.0 / 5040.0, 1.0 / 120.0, -1.0 / 6.0, 1.0):
        s = s * sq + c
    s = s * half
    c = 1.0 / 479001600.0
    for k in (-1.0 / 3628800.0, 1.0 / 40320.0, -1.0 / 720.0, 1.0 / 24.0, -0.5, 1.0):
        c = c * sq + k
    return 1.0 - 2.0 * s * s, 2.0 * s * c


def centred(index):
    return jnp.where(index >= HALF, index - N, index).astype(f32)


def unit_lanes(u):
    return slice(256 * u, 256 * u + (256 if u < 2 else 128))


def kernel(
    rot_hbm, counts_hbm, shifts, image, fwd_hbm, inv_hbm, fwd3_hbm, fz_hbm, gz_hbm,
    out,
    rot, counts, v, vt, fwd, inv, fwd3, fz, gz,
    cos_f, sin_f, cos_x, sin_x, cos_z, sin_z,
    xsend, xrecv, zsend, planes, rsend, rrecv, fsend, frecv,
    params, turned, second, total, packed, final,
    ready, image_sem, load_sem, xl_sem, zl_sem, ps_sem, pr_sem,
    xs_sem, xr_sem, zs_sem, zr_sem, ys_sem, yr_sem, fs_sem, fr_sem,
):
    state = lax.axis_index("state")
    slab = lax.axis_index("slab")
    zlo = state // 4
    y = state % 4
    zhi = slab // 8
    x = (slab % 8) // 2
    core = slab % 2
    me = slab % 8
    spot = zhi * 2 + zlo

    def image_load(i):
        part = pl.ds(2 * i, 2)
        return pltpu.make_async_copy(image.at[:, part], v.at[:, part], image_sem.at[i])

    loads = [
        pltpu.make_async_copy(src, dst, load_sem.at[i])
        for i, (src, dst) in enumerate(
            ((rot_hbm, rot), (counts_hbm, counts), (fwd_hbm, fwd), (inv_hbm, inv),
             (fz_hbm, fz), (gz_hbm, gz), (fwd3_hbm, fwd3))
        )
    ]
    for copy in loads[:2]:
        copy.start()
    for i in range(5):
        image_load(i).start()

    barrier = pltpu.get_barrier_semaphore()

    def ring(o):
        to = lax.rem(spot + o, RING)
        return {"state": (to % 2) * 4 + y, "slab": (to // 2) * 8 + me}

    for o in range(1, 8):
        pl.semaphore_signal(
            barrier, inc=1, device_id={"slab": zhi * 8 + lax.rem(me + o, 8)}, device_id_type=MESH)
    for o in range(1, RING):
        pl.semaphore_signal(barrier, inc=1, device_id=ring(o), device_id_type=MESH)
    for o in range(1, 4):
        pl.semaphore_signal(
            barrier, inc=1, device_id={"state": zlo * 4 + lax.rem(y + o, 4)}, device_id_type=MESH)
    for copy in loads[2:4]:
        copy.start()

    for copy in loads[:2]:
        copy.wait()
    tilt = shifts[0, rot[0]]
    lift = shifts[1, rot[0]]
    weight = counts[0].astype(f32) * (1.0 / 64.0)
    centre = (N - 1) / 2.0

    row = lax.broadcasted_iota(jnp.int32, (16, PAD), 0) + slab * 10
    freq = centred(lax.broadcasted_iota(jnp.int32, (16, PAD), 1)) * (1.0 / N)
    cosine, sine = turn(freq * (tilt * (row.astype(f32) - centre)))
    cos_f[...] = cosine
    sin_f[...] = sine

    row8 = lax.broadcasted_iota(jnp.int32, (8, 128), 0)
    params[zlo] = jnp.where(row8 == 0, tilt, jnp.where(row8 == 1, lift, weight))
    swap_params = pltpu.make_async_remote_copy(
        src_ref=params.at[zlo], dst_ref=params.at[zlo], send_sem=ps_sem, recv_sem=pr_sem,
        device_id={"state": (1 - zlo) * 4 + y}, device_id_type=MESH)

    def turn_image(i, _):
        image_load(i).wait()
        for coef in range(2):
            for j in range(2):
                vt[coef, 2 * i + j] = v[coef, 2 * i + j].T
        return 0

    lax.fori_loop(0, 5, turn_image, 0)
    for copy in loads[2:4]:
        copy.wait()

    def chunk_y(t):
        return lax.rem(y + 1 + t, 4)

    def first(t):
        yy = chunk_y(t)
        left = jnp.concatenate(
            [vt[coef, z, pl.ds(pl.multiple_of(64 * low + 16 * yy, 16), 16), :]
             for z in range(10) for coef in range(2) for low in range(2)], axis=0)
        spectrum = jnp.dot(left, fwd[...], preferred_element_type=f32)
        ramped = []
        for z in range(10):
            cosine = jnp.broadcast_to(cos_f[z : z + 1, :], (64, PAD))
            sine = jnp.broadcast_to(sin_f[z : z + 1, :], (64, PAD))
            re = spectrum[64 * z : 64 * (z + 1), :PAD]
            im = spectrum[64 * z : 64 * (z + 1), PAD:]
            ramped.append(
                jnp.concatenate([re * cosine + im * sine, im * cosine - re * sine], axis=1).astype(bf16))
        moved = jnp.dot(jnp.concatenate(ramped, axis=0), inv[...], preferred_element_type=f32)
        for pair in range(5):
            for coef in range(2):
                for low in range(2):
                    for h in range(2):
                        q = 128 * pair + 32 * coef + 16 * low + 8 * h
                        piece = jnp.concatenate([moved[q : q + 8], moved[q + 64 : q + 72]], axis=0)
                        xsend[(coef * 2 + h) * 2 + low, t, 16 * pair : 16 * (pair + 1), :] = piece.astype(bf16)

    def x_copies(t, u):
        lanes = unit_lanes(u)
        lanes = pl.ds(lanes.start, lanes.stop - lanes.start)
        out_copies = []
        for o in range(1, 8):
            gx = lax.rem(x + o // 2, 4)
            gc = lax.rem(core + o, 2)
            out_copies.append(pltpu.make_async_remote_copy(
                src_ref=xsend.at[gx * 2 + gc, t, :, lanes], dst_ref=xrecv.at[t, me, :, lanes],
                send_sem=xs_sem.at[t, u, o - 1], recv_sem=xr_sem.at[t, u, o - 1],
                device_id={"slab": zhi * 8 + gx * 2 + gc}, device_id_type=MESH))
        return out_copies, lambda: pltpu.make_async_copy(
            xsend.at[me, t, :, lanes], xrecv.at[t, me, :, lanes], xl_sem.at[t, u])

    def z_copies(t, u):
        lanes = unit_lanes(u)
        lanes = pl.ds(lanes.start, lanes.stop - lanes.start)
        out_copies = []
        dst = planes.at[t, zlo, pl.ds(pl.multiple_of(zhi * BLOCK, 16), BLOCK), lanes]
        for o in (4, 3, 5, 2, 6, 1, 7):
            to = lax.rem(spot + o, RING)
            out_copies.append(pltpu.make_async_remote_copy(
                src_ref=zsend.at[t, to, :, lanes], dst_ref=dst,
                send_sem=zs_sem.at[t, u, o - 1], recv_sem=zr_sem.at[t, u, o - 1],
                device_id={"state": (to % 2) * 4 + y, "slab": (to // 2) * 8 + me}, device_id_type=MESH))
        return out_copies, lambda: pltpu.make_async_copy(zsend.at[t, spot, :, lanes], dst, zl_sem.at[t, u])

    def y_copy(t):
        return pltpu.make_async_remote_copy(
            src_ref=rsend.at[t], dst_ref=rrecv.at[t],
            send_sem=ys_sem.at[t], recv_sem=yr_sem.at[t],
            device_id={"state": zlo * 4 + chunk_y(t)}, device_id_type=MESH)

    def start(copies):
        remote, own = copies
        for copy in remote:
            copy.start()
        own().start()

    def arrive(copies):
        remote, own = copies
        own().wait()
        for copy in remote:
            copy.wait_recv()

    first(0)
    pl.semaphore_wait(barrier, 2 * 7 + 3)
    start(x_copies(0, UNITS[0]))
    swap_params.start()
    start(x_copies(0, UNITS[1]))
    for o in range(1, RING):
        pl.semaphore_signal(ready, inc=1, device_id=ring(o), device_id_type=MESH)
    for copy in loads[4:]:
        copy.start()

    def tables(i, _):
        row = lax.broadcasted_iota(jnp.int32, (16, 128), 0) + i * 16
        for s in range(2):
            rows = pl.ds(pl.multiple_of(s * N + i * 16, 16), 16)
            tilt_s = params[s, 0:1, :]
            lift_s = params[s, 1:2, :]
            for tile in range(3):
                lanes = slice(128 * tile, 128 * (tile + 1))
                lane = lax.broadcasted_iota(jnp.int32, (16, 128), 1) + 128 * tile
                cosine, sine = turn(centred(lane) * (tilt_s * (row.astype(f32) - centre)) * (1.0 / N))
                cos_x[rows, lanes] = cosine
                sin_x[rows, lanes] = sine
                at = jnp.where(lane >= N, lane - 64, lane)
                cosine, sine = turn(centred(row) * (lift_s * (at.astype(f32) - centre)) * (1.0 / N))
                cos_z[rows, lanes] = cosine
                sin_z[rows, lanes] = sine
        return 0

    def transpose(t, u):
        lanes = unit_lanes(u)
        for lane in range(lanes.start // 128, lanes.stop // 128):
            for g in range(8):
                turned[lane, BLOCK * g : BLOCK * (g + 1), :] = xrecv[
                    t, g, :, 128 * lane : 128 * (lane + 1)].astype(f32)
        for lane in range(lanes.start // 128, lanes.stop // 128):
            for m in range(8):
                zsend[t, m, :, 128 * lane : 128 * (lane + 1)] = turned[
                    lane, pl.ds(m, BLOCK, stride=8), :].astype(bf16)

    lane128 = lax.broadcasted_iota(jnp.int32, (N, 128), 1)

    def swap(left, right, paired):
        if paired:
            return right, -left
        l = pltpu.roll(left, 64, 1)
        r = pltpu.roll(right, 64, 1)
        return jnp.where(lane128 < 64, l, -l), jnp.where(lane128 < 64, r, -r)

    def shear_z(t, u):
        if u < 2:
            pairs = [((s, 2 * u), (s, 2 * u + 1)) for s in range(2)]
        else:
            pairs = [((0, 4), (1, 4))]
        for pair in pairs:
            data = jnp.concatenate([planes[t, s, :, 128 * b : 128 * (b + 1)] for s, b in pair], axis=1)
            both = jnp.dot(fz[...], data, preferred_element_type=f32)
            near, far = [], []
            for i, (s, b) in enumerate(pair):
                cosine = cos_z[s * N : (s + 1) * N, 128 * u : 128 * (u + 1)]
                sine = sin_z[s * N : (s + 1) * N, 128 * u : 128 * (u + 1)]
                tc = both[:N, 128 * i : 128 * (i + 1)]
                ts = both[N:, 128 * i : 128 * (i + 1)]
                near.append(cosine * tc - sine * ts)
                far.append(cosine * ts + sine * tc)
            far = swap(far[0], far[1], u < 2)
            ramped = jnp.concatenate([near[0] + far[0], near[1] + far[1]], axis=1).astype(bf16)
            both = jnp.dot(gz[...], ramped, preferred_element_type=f32)
            far = swap(both[N:, :128], both[N:, 128:], u < 2)
            for i, (s, b) in enumerate(pair):
                second[s * N : (s + 1) * N, 128 * b : 128 * (b + 1)] = (
                    both[:N, 128 * i : 128 * (i + 1)] - far[i]).astype(bf16)

    def shear_x(t, half):
        here = pl.ds(pl.multiple_of(160 * half, 16), 160)
        there = pl.ds(pl.multiple_of(N + 160 * half, 16), 160)
        left = jnp.concatenate([second[here, :], second[there, :]], axis=0)
        spectrum = jnp.dot(left, fwd3[...], preferred_element_type=f32)
        re, im = spectrum[:, :PAD], spectrum[:, PAD:]
        cosine = jnp.concatenate([cos_x[here, :], cos_x[there, :]], axis=0)
        sine = jnp.concatenate([sin_x[here, :], sin_x[there, :]], axis=0)
        ramped = jnp.concatenate([re * cosine + im * sine, im * cosine - re * sine], axis=1).astype(bf16)
        moved = jnp.dot(ramped, inv[...], preferred_element_type=f32)
        w0 = jnp.concatenate([params[0, 2:3, :]] * 5, axis=1)
        w1 = jnp.concatenate([params[1, 2:3, :]] * 5, axis=1)
        rsend[t, here, :] = (moved[:160] * w0 + moved[160:] * w1).astype(bf16)

    def step(t, _):
        @pl.when(t < CHUNKS)
        def _():
            for i, u in enumerate(UNITS):
                arrive(x_copies(t, u))
                transpose(t, u)
                start(z_copies(t, u))
                if i == 0:
                    @pl.when(t == 0)
                    def _():
                        start(x_copies(0, UNITS[2]))

                    @pl.when(t < CHUNKS - 1)
                    def _():
                        first(t + 1)

                @pl.when(t < CHUNKS - 1)
                def _():
                    start(x_copies(t + 1, u))

        @pl.when(t == 0)
        def _():
            swap_params.wait()
            for copy in loads[4:]:
                copy.wait()
            lax.fori_loop(0, N // 16, tables, 0)

        @pl.when(t >= 1)
        def _():
            for u in UNITS:
                arrive(z_copies(t - 1, u))
                shear_z(t - 1, u)

            @pl.when(t < CHUNKS)
            def _():
                shear_x(t - 1, 0)
                shear_x(t - 1, 1)
                y_copy(t - 1).start()

        return 0

    lax.fori_loop(0, CHUNKS + 1, step, 0)
    for t in range(CHUNKS - 1):
        y_copy(t).wait_recv()

    target = core * 4 + y
    slot = x * RING + spot
    for g in range(8):
        packed[g, FILLED:PACKED, :] = jnp.zeros((PACKED - FILLED, 128), f32)

    def f_copy(to):
        return pltpu.make_async_remote_copy(
            src_ref=fsend.at[to], dst_ref=frecv.at[slot],
            send_sem=fs_sem.at[to], recv_sem=fr_sem.at[slot],
            device_id={"state": target, "slab": to}, device_id_type=MESH)

    def is_own(to):
        return jnp.logical_and(to == slab, target == state)

    def pack(i, _):
        block = 2 * lax.rem(zhi // 2 + 1 + i // 2, 2) + lax.rem(zhi + i, 2)
        rows = pl.ds(pl.multiple_of(block * BLOCK, 16), BLOCK)
        for b in range(5):
            lanes = slice(128 * b, 128 * (b + 1))
            acc = rsend[CHUNKS - 1, rows, lanes].astype(f32)
            for t in range(CHUNKS - 1):
                acc = acc + rrecv[t, rows, lanes].astype(f32)
            total[b] = acc
        for g in range(8):
            to = block * 8 + g
            for b in range(5):
                packed[g, b * 10 : b * 10 + 10, :] = total[b, 10 * g : 10 * g + 10, :]
            fsend[to] = packed[g].astype(bf16)

            @pl.when(is_own(to))
            def _():
                pltpu.make_async_copy(fsend.at[slab], frecv.at[slot], fr_sem.at[slot]).start()

            @pl.when(jnp.logical_not(is_own(to)))
            def _():
                f_copy(to).start()

        return 0

    pl.semaphore_wait(ready, RING - 1)


    def finish(i, _):
        shear_x(CHUNKS - 1, lax.rem(zhi // 2 + 1 + i, 2))
        lax.fori_loop(2 * i, 2 * i + 2, pack, 0)
        return 0

    lax.fori_loop(0, 2, finish, 0)

    def sent(t, _):
        for u in range(3):
            for copy in x_copies(t, u)[0] + z_copies(t, u)[0]:
                copy.wait_send()
        return 0

    lax.fori_loop(0, CHUNKS, sent, 0)
    for t in range(CHUNKS - 1):
        y_copy(t).wait_send()

    def left(to, _):
        @pl.when(jnp.logical_not(is_own(to)))
        def _():
            f_copy(to).wait_send()

        return 0

    lax.fori_loop(0, 32, left, 0)

    for source in range(4):
        for at in range(RING):
            i = source * RING + at
            pltpu.make_async_copy(fsend.at[0], frecv.at[i], fr_sem.at[i]).wait()
            final[source, PACKED * at : PACKED * (at + 1), :] = frecv[i].astype(f32)
        for z in range(10):
            for b in range(5):
                rows = final[source, pl.ds(b * 10 + z, RING, stride=PACKED), :]
                base = (source // 2) * N + 32 * z + 8 * (source % 2)
                if b < 4:
                    base += 16 * (b % 2)
                    out[base : base + 8, 128 * (b // 2) : 128 * (b // 2 + 1)] = rows
                else:
                    out[base : base + 8, 256:320] = rows[:, :64]
                    out[base + 16 : base + 24, 256:320] = pltpu.roll(rows, 64, 1)[:, :64]


def body(state_images, rot_index, counts):
    fwd, inv, fwd3, fz, gz, shifts = host_tables()
    image = state_images.reshape(2, 10, 2 * N, 128)
    smem = pl.BlockSpec(memory_space=pltpu.SMEM)
    anywhere = pl.BlockSpec(memory_space=pl.ANY)
    dma = pltpu.SemaphoreType.DMA
    vmem = pltpu.VMEM
    out = pl.pallas_call(
        kernel,
        name="shears",
        out_shape=jax.ShapeDtypeStruct((640, N), f32),
        in_specs=[anywhere, anywhere, smem] + [anywhere] * 6,
        out_specs=pl.BlockSpec(memory_space=vmem),
        scratch_shapes=[
            pltpu.SMEM((1,), jnp.int32), pltpu.SMEM((1,), jnp.int32),
            vmem(image.shape, bf16), vmem((2, 10, 128, LANES), bf16), vmem(fwd.shape, bf16), vmem(inv.shape, bf16),
            vmem(fwd3.shape, bf16), vmem(fz.shape, bf16), vmem(gz.shape, bf16),
            vmem((16, PAD), f32), vmem((16, PAD), f32),
            vmem((2 * N, PAD), f32), vmem((2 * N, PAD), f32), vmem((2 * N, PAD), f32), vmem((2 * N, PAD), f32),
            vmem((8, 4, BLOCK, LANES), bf16),
            vmem((CHUNKS, 8, BLOCK, LANES), bf16),
            vmem((CHUNKS, RING, BLOCK, LANES), bf16),
            vmem((CHUNKS, 2, N, LANES), bf16),
            vmem((CHUNKS, N, LANES), bf16),
            vmem((CHUNKS - 1, N, LANES), bf16),
            vmem((32, PACKED, 128), bf16),
            vmem((32, PACKED, 128), bf16),
            vmem((2, 8, 128), f32),
            vmem((5, 640, 128), f32),
            vmem((2 * N, LANES), bf16),
            vmem((5, BLOCK, 128), f32),
            vmem((8, PACKED, 128), f32),
            vmem((4, RING * PACKED, 128), f32),
            pltpu.SemaphoreType.REGULAR, dma((5,)), dma((7,)), dma((CHUNKS, 3)), dma((CHUNKS, 3)), dma, dma,
            dma((CHUNKS, 3, 7)), dma((CHUNKS, 3, 7)),
            dma((CHUNKS, 3, RING - 1)), dma((CHUNKS, 3, RING - 1)),
            dma((CHUNKS - 1,)), dma((CHUNKS - 1,)),
            dma((32,)), dma((32,)),
        ],
        compiler_params=pltpu.CompilerParams(
            collective_id=0, has_side_effects=True, vmem_limit_bytes=60 * 1024 * 1024),
        cost_estimate=pl.CostEstimate(flops=13_000_000_000, bytes_accessed=8_000_000, transcendentals=0),
    )(rot_index, counts, shifts, image, fwd, inv, fwd3, fz, gz)
    return out.reshape(2, 10, 2, 16, N).swapaxes(3, 4)


def solution(mesh):
    placed = (P("state", None, "slab", None, None, None), P("state"), P("state"))
    return jax.shard_map(
        body,
        mesh=mesh,
        in_specs=placed,
        out_specs=P(None, "slab", None, None, "state"),
        check_vma=False,
    )
```
